512 devices in a mesh: dst: 32 (over z, y_lo), src: 16 (over x, y_hi, core).
Axes of the slice: x: 4, y: 8 (y_hi: 2, y_lo: 4; y = y_hi * 4 + y_lo), z: 8, core: 2. Of those that a mesh axis runs over, the one named last changes fastest.
Arguments:
- node_features: bfloat16 [64, 196608], P(None, ('dst', 'src')), may hold values from -6 to 6
- edge_values: bfloat16 [32, 16, 8, 128, 128], P('dst', 'src'), may hold values from 0 to 2, as said below
- tile_rows: int32 [32, 16, 8], P('dst', 'src'), may hold values from 0 to 47, as said below
- tile_cols: int32 [32, 16, 8], P('dst', 'src'), may hold values from 0 to 95
- a_weight: bfloat16 [64, 64], replicated, may hold values from -0.75 to 0.75
- b_weight: bfloat16 [64, 64], replicated, may hold values from -1.5 to 1.5
- d_weight: bfloat16 [64, 64], replicated, may hold values from -0.75 to 0.75
- e_weight: bfloat16 [64, 64], replicated, may hold values from -0.75 to 0.75
- edge_gain: float32 [64], replicated, may hold values from -4 to 4
- ln_gain: float32 [64], replicated, may hold values from 0.1 to 1.9
Outputs:
- new_features: bfloat16 [64, 196608], P(None, ('dst', 'src'))
The draws below stay inside these ranges and needn't reach their ends.
Inputs may be any that keep to these rules, and one draw needn't show every extreme that they name: Within one device the pairs (tile_rows, tile_cols) are all different. All tiles of one device whose tile_rows have the same value of tile_rows // 3 have the same tile_rows. Each device has a number of live tiles, from 8 / 2 (rounded down) up to 8, at least one device having 8; its slots past that number hold only zeros in edge_values. `edge_values`: live tiles have about one entry in 20 nonzero; nonzero entries lie between 0.5 and 2.
All inputs are finite; a program needn't handle non-finite values.
Results may differ from the reference program's by a relative error of at most 0.007.
Values may be sent and summed in bfloat16 or wider, within the bound.
No kernel may reach another device: no remote copies, remote signals or barrier semaphores. Data moves between devices by JAX's collectives and lax.ppermute only.
A program may use at most 64 MiB of HBM per device.

```python
import jax
import jax.numpy as jnp
from jax import lax

WIDTH = 64
BLOCK = 128
SHARD = 384
TILES = 8
NODES = 196608
N_DST = 32
N_SRC = 16


def tile_layout(key):
    shard_blocks = SHARD // BLOCK
    col_blocks = N_DST * shard_blocks
    device_count = N_DST * N_SRC
    base = jax.random.fold_in(key, 11)
    block_key, owner_key, perm_key, full_key, some_key = jax.random.split(base, 5)
    device_index = jnp.arange(device_count, dtype=jnp.int32)
    local_block = jax.random.randint(block_key, (device_count, N_SRC), 0, shard_blocks).astype(jnp.int32)
    owner_pick = jax.random.randint(owner_key, (device_count, TILES), 0, N_SRC).astype(jnp.int32)
    local_block = jnp.where((device_index == 0)[:, None], shard_blocks - 1, local_block)
    local_block = jnp.where((device_index == 1)[:, None], 0, local_block)
    owner_pick = owner_pick.at[0, 0].set(N_SRC - 1)
    owner_pick = owner_pick.at[1, 0].set(0)
    block_pick = jnp.take_along_axis(local_block, owner_pick, axis=1)
    rows_flat = owner_pick * shard_blocks + block_pick
    perm_keys = jax.random.split(perm_key, device_count)

    def choose(one_key):
        return jax.random.permutation(one_key, col_blocks)[:TILES].astype(jnp.int32)
    perms = jax.vmap(choose)(perm_keys)
    target = jnp.where(device_index == 0, col_blocks - 1, 0).astype(jnp.int32)
    shift_by = jnp.where(device_index < 2, target - perms[:, 0], 0).astype(jnp.int32)
    cols_flat = (perms + shift_by[:, None] + col_blocks) % col_blocks
    chosen = jax.random.randint(full_key, (), 0, device_count)
    some_count = jax.random.randint(some_key, (device_count,), TILES // 2, TILES + 1)
    live_count = jnp.where(device_index == chosen, TILES, some_count).astype(jnp.int32)
    rows_out = rows_flat.reshape(N_DST, N_SRC, TILES)
    cols_out = cols_flat.reshape(N_DST, N_SRC, TILES)
    return (rows_out, cols_out, live_count.reshape(N_DST, N_SRC))


def draw_tile_rows(key, part):
    rows_out, cols_out, live_count = tile_layout(key)
    return rows_out.astype(jnp.int32)


def draw_tile_cols(key, part):
    rows_out, cols_out, live_count = tile_layout(key)
    return cols_out.astype(jnp.int32)


def draw_edge_values(key, part):
    rows_out, cols_out, live_count = tile_layout(key)
    own_key = jax.random.fold_in(key, 5)
    mask_key, value_key = jax.random.split(own_key)
    shape_all = (N_DST, N_SRC, TILES, BLOCK, BLOCK)
    edge_flag = jax.random.randint(mask_key, shape_all, 0, 20) == 0
    edge_feats = jax.random.uniform(value_key, shape_all, jnp.float32, 0.5, 2.0)
    live_flag = jnp.arange(TILES, dtype=jnp.int32)[None, None, :] < live_count[:, :, None]
    keep = edge_flag & live_flag[:, :, :, None, None]
    return jnp.where(keep, edge_feats, 0.0).astype(jnp.bfloat16)


def levels(stream_key, extent, shards, low, high):
    def one(dim, parts):
        heights = jax.random.uniform(jax.random.fold_in(jax.random.fold_in(stream_key, 6), dim), (parts,), jnp.float32, low / len(shards), high / len(shards))
        return jnp.repeat(jnp.exp(heights), extent[dim] // parts).reshape((-1,) + (1,) * (len(extent) - dim - 1))

    level = one(*shards[0])
    for cut in shards[1:]:
        level = level * one(*cut)
    return level


def gaussian(rng, dims, scale, reach, shards=(), kind=jnp.bfloat16):
    array = scale * jax.random.normal(rng, dims, jnp.float32)
    if shards:
        array = array * levels(rng, dims, shards, -0.22, 0.18)
    return jnp.clip(array, -reach, reach).astype(kind)


def setup_inputs(seed: int = 0) -> dict:
    splits = jax.random.split(jax.random.key(seed), 11)
    return {
        "node_features": gaussian(splits[0], (WIDTH, NODES), 1.0, 6.0, ((1, 512),)),
        "edge_values": draw_edge_values(jax.random.fold_in(splits[10], 71), 0),
        "tile_rows": draw_tile_rows(jax.random.fold_in(splits[10], 71), 0),
        "tile_cols": draw_tile_cols(jax.random.fold_in(splits[10], 71), 0),
        "a_weight": gaussian(splits[4], (WIDTH, WIDTH), WIDTH ** -0.5, 0.75),
        "b_weight": gaussian(splits[5], (WIDTH, WIDTH), 0.25, 1.5),
        "d_weight": gaussian(splits[6], (WIDTH, WIDTH), WIDTH ** -0.5, 0.75),
        "e_weight": gaussian(splits[7], (WIDTH, WIDTH), WIDTH ** -0.5, 0.75),
        "edge_gain": gaussian(splits[8], (WIDTH,), 1.0, 4.0, (), jnp.float32),
        "ln_gain": jnp.clip(1.0 + 0.18 * jax.random.normal(splits[9], (WIDTH,), jnp.float32), 0.1, 1.9),
    }


def tile_terms(row_gate, col_gate, col_value, values, edge_gain):
    values_f = values.astype(jnp.float32)
    preact = row_gate.astype(jnp.float32)[:, :, None] + col_gate.astype(jnp.float32)[:, None, :] + edge_gain[:, None, None] * values_f[None]
    gate_vals = jax.nn.sigmoid(preact) * (values != 0).astype(jnp.float32)[None]
    numerator = jnp.einsum('fij,fj->fi', gate_vals, col_value.astype(jnp.float32))
    denominator = lax.optimization_barrier(jnp.sum(gate_vals, axis=2))
    return (numerator, denominator)

def finish(features, a_proj, numerator, denominator, ln_gain):
    mixed = a_proj + numerator / (denominator + 1e-06)
    center = mixed - lax.optimization_barrier(jnp.mean(mixed, axis=0, keepdims=True))
    spread = lax.optimization_barrier(jnp.mean(center * center, axis=0, keepdims=True))
    normed = center * lax.rsqrt(spread + 1e-05) * ln_gain[:, None]
    return (features.astype(jnp.float32) + jax.nn.relu(normed)).astype(jnp.bfloat16)

def reference(node_features, edge_values, tile_rows, tile_cols, a_weight, b_weight, d_weight, e_weight, edge_gain, ln_gain):
    a_proj = jnp.dot(a_weight, node_features, preferred_element_type=jnp.float32)
    b_proj = jnp.dot(b_weight, node_features, preferred_element_type=jnp.float32).astype(jnp.bfloat16)
    d_proj = jnp.dot(d_weight, node_features, preferred_element_type=jnp.float32).astype(jnp.bfloat16)
    e_proj = jnp.dot(e_weight, node_features, preferred_element_type=jnp.float32).astype(jnp.bfloat16)
    values_all = edge_values.reshape(-1, BLOCK, BLOCK)
    rows_all = tile_rows.reshape(-1).astype(jnp.int32)
    cols_all = tile_cols.reshape(-1).astype(jnp.int32)
    order = jnp.arange(N_DST * N_SRC * TILES, dtype=jnp.int32)
    dst_index = order // (N_SRC * TILES)
    src_index = order // TILES % N_SRC
    shard_blocks = SHARD // BLOCK
    row_starts = (dst_index * (N_SRC * SHARD) + rows_all * BLOCK).astype(jnp.int32)
    col_starts = ((cols_all // shard_blocks * N_SRC + src_index) * SHARD + cols_all % shard_blocks * BLOCK).astype(jnp.int32)
    zero_index = jnp.zeros((), jnp.int32)

    def add_tile(totals, tile_item):
        numerator, denominator = totals
        values, row_start, col_start = tile_item
        row_gate = lax.dynamic_slice(d_proj, (zero_index, row_start), (WIDTH, BLOCK))
        col_gate = lax.dynamic_slice(e_proj, (zero_index, col_start), (WIDTH, BLOCK))
        col_value = lax.dynamic_slice(b_proj, (zero_index, col_start), (WIDTH, BLOCK))
        part_num, part_den = tile_terms(row_gate, col_gate, col_value, values, edge_gain)
        old_num = lax.dynamic_slice(numerator, (zero_index, row_start), (WIDTH, BLOCK))
        old_den = lax.dynamic_slice(denominator, (zero_index, row_start), (WIDTH, BLOCK))
        numerator = lax.dynamic_update_slice(numerator, old_num + part_num, (zero_index, row_start))
        denominator = lax.dynamic_update_slice(denominator, old_den + part_den, (zero_index, row_start))
        return ((numerator, denominator), None)
    start_sums = (jnp.zeros((WIDTH, NODES), jnp.float32), jnp.zeros((WIDTH, NODES), jnp.float32))
    (numerator, denominator), _ = lax.scan(add_tile, start_sums, (values_all, row_starts, col_starts))
    return finish(node_features, a_proj, numerator, denominator, ln_gain)
```

```python
import jax, jax.numpy as jnp
from jax import lax
from jax.sharding import Mesh, PartitionSpec as P
from jax.experimental import pallas as pl
from jax.experimental.pallas import tpu as pltpu

GROUP = 8

def tiles_kernel(owner_ref, row_ref, block_ref, col_ref, gain_ref, rows_ref, cols_ref, w_ref, wd_ref, we_ref, wb_ref,
                 out_ref, acc, gates, d_scr, b_scr, wt_scr, mask_scr):
    n_tiles, block_len, _ = w_ref.shape
    width = wd_ref.shape[0]
    n_groups = width // GROUP
    acc[...] = jnp.zeros_like(acc)
    out_ref[:, 2 * width:, :] = jnp.zeros((out_ref.shape[0], 16, block_len), out_ref.dtype)
    row_id = lax.broadcasted_iota(jnp.int32, (2 * GROUP, block_len), 0)

    def tile(t, _):
        owner = owner_ref[t]
        xr = rows_ref[row_ref[t]]
        xc = cols_ref[col_ref[t]]
        half = jnp.float32(0.5)
        d_scr[...] = half * jnp.dot(wd_ref[...], xr, preferred_element_type=jnp.float32).astype(jnp.bfloat16).astype(jnp.float32)
        b_scr[...] = jnp.dot(wb_ref[...], xc, preferred_element_type=jnp.float32).astype(jnp.bfloat16).astype(jnp.float32)
        wt = w_ref[t].astype(jnp.float32).T
        wt_scr[...] = half * wt
        mask_scr[...] = (wt != 0).astype(jnp.float32)

        def group(g, _):
            we_g = we_ref[pl.ds(pl.multiple_of(g * GROUP, GROUP), GROUP), :]
            e_t = lax.dot_general(xc, we_g, (((0,), (1,)), ((), ())), preferred_element_type=jnp.float32)
            e_t = half * e_t.astype(jnp.bfloat16).astype(jnp.float32)
            d_g = d_scr[pl.ds(pl.multiple_of(g * GROUP, GROUP), GROUP), :]
            b_g = b_scr[pl.ds(pl.multiple_of(g * GROUP, GROUP), GROUP), :]
            lhs = []
            for k in range(GROUP):
                p = gain_ref[g * GROUP + k] * wt_scr[...] + d_g[k:k + 1, :] + e_t[:, k:k + 1]
                s = (jnp.tanh(p) + 1.0) * mask_scr[...]
                gates[k * block_len:(k + 1) * block_len, :] = s.astype(jnp.bfloat16)
                lhs.append(jnp.where(row_id == k, b_g[k:k + 1, :], jnp.where(row_id == GROUP + k, 1.0, 0.0)).astype(jnp.bfloat16))
            lhs = jnp.concatenate(lhs, axis=1)
            sums = jnp.dot(lhs, gates[...], preferred_element_type=jnp.float32)
            at = pl.ds(pl.multiple_of(g * GROUP, GROUP), GROUP)
            acc[owner, at, :] += half * sums[:GROUP]
            at2 = pl.ds(pl.multiple_of(width + g * GROUP, GROUP), GROUP)
            acc[owner, at2, :] += half * sums[GROUP:]
            return 0
        lax.fori_loop(0, n_groups, group, 0)
        out_ref[owner, 2 * width:, :] = jnp.full((16, block_len), block_ref[t], jnp.int32).astype(jnp.float32).astype(out_ref.dtype)
        return 0
    lax.fori_loop(0, n_tiles, tile, 0)
    out_ref[:, :2 * width, :] = acc[...].astype(out_ref.dtype)


def tile_sums(owner, row, block, col, gain, rows, cols, w, wd, we, wb, n_owners):
    n_tiles, block_len, _ = w.shape
    width = wd.shape[0]
    smem = pl.BlockSpec(memory_space=pltpu.SMEM)
    vmem = pl.BlockSpec(memory_space=pltpu.VMEM)
    return pl.pallas_call(
        tiles_kernel,
        out_shape=jax.ShapeDtypeStruct((n_owners, 2 * width + 16, block_len), jnp.bfloat16),
        in_specs=[smem] * 5 + [vmem] * 6,
        out_specs=vmem,
        scratch_shapes=[
            pltpu.VMEM((n_owners, 2 * width, block_len), jnp.float32),
            pltpu.VMEM((GROUP * block_len, block_len), jnp.bfloat16),
            pltpu.VMEM((width, block_len), jnp.float32),
            pltpu.VMEM((width, block_len), jnp.float32),
            pltpu.VMEM((block_len, block_len), jnp.float32),
            pltpu.VMEM((block_len, block_len), jnp.float32),
        ],
        compiler_params=pltpu.CompilerParams(vmem_limit_bytes=32 * 1024 * 1024),
        name="tile_sums",
    )(owner, row, block, col, gain, rows, cols, w, wd, we, wb)


def finish_kernel(parts_ref, x_ref, wa_ref, gain_ref, out_ref):
    width = wa_ref.shape[0]
    n_src, _, block_len = parts_ref.shape
    n_blocks = x_ref.shape[1] // block_len
    for k in range(n_blocks):
        num = jnp.zeros((width, block_len), jnp.float32)
        den = jnp.zeros((width, block_len), jnp.float32)
        for s in range(n_src):
            hit = (parts_ref[s, 2 * width:, :].astype(jnp.float32)[:1] == float(k)).astype(jnp.float32)
            num += parts_ref[s, :width, :].astype(jnp.float32) * hit
            den += parts_ref[s, width:2 * width, :].astype(jnp.float32) * hit
        x = x_ref[:, k * block_len:(k + 1) * block_len]
        a = jnp.dot(wa_ref[...], x, preferred_element_type=jnp.float32)
        mixed = a + num / (den + 1e-6)
        center = mixed - jnp.mean(mixed, axis=0, keepdims=True)
        spread = jnp.mean(center * center, axis=0, keepdims=True)
        normed = center * lax.rsqrt(spread + 1e-5) * gain_ref[...]
        out_ref[:, k * block_len:(k + 1) * block_len] = (x.astype(jnp.float32) + jnp.maximum(normed, 0.0)).astype(jnp.bfloat16)


def finish(parts, x, wa, gain):
    vmem = pl.BlockSpec(memory_space=pltpu.VMEM)
    return pl.pallas_call(
        finish_kernel,
        out_shape=jax.ShapeDtypeStruct(x.shape, jnp.bfloat16),
        in_specs=[vmem] * 4, out_specs=vmem,
        name="finish",
    )(parts, x, wa, gain[:, None])


def spread(x, axes, n):
    return lax.all_to_all(jnp.broadcast_to(x[None], (n,) + x.shape), axes, 0, 0)


def local(x, edge_values, tile_rows, tile_cols, wa, wb, wd, we, edge_gain, ln_gain):
    width, shard = x.shape
    n_tiles, block_len = edge_values.shape[-3], edge_values.shape[-1]
    n_blocks = shard // block_len
    n_z, n_y, n_x, n_h, n_c = (lax.axis_size(a) for a in AXES)
    n_src = n_x * n_h * n_c
    rows, cols = tile_rows.reshape(-1), tile_cols.reshape(-1)
    tiles = edge_values.reshape(n_tiles, block_len, block_len)
    blocks = x.reshape(width, n_blocks, block_len).transpose(1, 0, 2)

    partner = lax.ppermute(blocks, "yhi", [(i, (i + 1) % n_h) for i in range(n_h)])
    by_z = spread(blocks, "z", n_z).reshape(n_z * n_blocks, width, block_len)
    wanted = spread(cols, "ylo", n_y)
    both = jnp.stack([blocks, partner])
    row_panel = spread(both, ("x", "core"), n_x * n_c)
    owner, block = wanted // n_blocks, wanted % n_blocks
    picked = jnp.take(by_z, ((owner // n_y) * n_blocks + block).reshape(-1), axis=0)
    col_blocks = lax.all_to_all(picked.reshape(n_y, n_tiles, width, block_len), "ylo", 0, 0)

    row_owner, row_block = rows // n_blocks, rows % n_blocks
    h = row_owner // n_c % n_h
    other = (h != lax.axis_index("yhi")).astype(jnp.int32)
    row_at = (((row_owner // (n_h * n_c)) * n_c + row_owner % n_c) * n_h + other) * n_blocks + row_block
    col_at = (cols // n_blocks % n_y) * n_tiles + jnp.arange(n_tiles, dtype=jnp.int32)
    parts = tile_sums(
        row_owner, row_at, row_block, col_at, edge_gain,
        row_panel.reshape(-1, width, block_len), col_blocks.reshape(-1, width, block_len),
        tiles, wd, we, wb, n_src,
    )
    parts = lax.all_to_all(parts, SRC, 0, 0)
    return finish(parts, x, wa, ln_gain)


AXES = ("z", "ylo", "x", "yhi", "core")
DST, SRC = AXES[:2], AXES[2:]


def solution(mesh):
    n_dst, n_src = mesh.devices.shape
    fine = Mesh(mesh.devices.reshape(n_dst // 4, 4, n_src // 4, 2, 2), AXES)
    in_specs = (
        P(None, AXES), P(DST, SRC, None, None, None), P(DST, SRC, None), P(DST, SRC, None),
        P(), P(), P(), P(), P(), P(),
    )
    return jax.shard_map(local, mesh=fine, in_specs=in_specs, out_specs=P(None, AXES), check_vma=False)
```

```python
import jax, jax.numpy as jnp
from jax import lax
from jax.sharding import Mesh, PartitionSpec as P
from jax.experimental import pallas as pl
from jax.experimental.pallas import tpu as pltpu

AXES = ("za", "zb", "ya", "yb", "x", "yhi", "core")
DST, SRC = AXES[:4], AXES[4:]
GROUP = 8
CHUNK = 128
BAND = 16


def pack_kernel(rows_ref, x_ref, shard_ref, spread_ref):
    width, shard = x_ref.shape
    block_len = spread_ref.shape[3]
    n_tiles = rows_ref.shape[0]
    for k in range(shard // block_len):
        block = x_ref[:, k * block_len:(k + 1) * block_len]
        shard_ref[k * width:(k + 1) * width, :] = block
        for n in range(spread_ref.shape[0]):
            spread_ref[n, k] = block
    sub = lax.broadcasted_iota(jnp.int32, (BAND, block_len), 0)
    band = jnp.full((BAND, block_len), -1, jnp.int32)
    for t in range(n_tiles):
        band = jnp.where(sub == t, rows_ref[t], band)
    shard_ref[shard // block_len * width:, :] = band.astype(jnp.float32).astype(shard_ref.dtype)


def pack(rows, x, block_len, copies):
    width, shard = x.shape
    n_blocks = shard // block_len
    vmem = pl.BlockSpec(memory_space=pltpu.VMEM)
    return pl.pallas_call(
        pack_kernel,
        out_shape=(
            jax.ShapeDtypeStruct((n_blocks * width + BAND, block_len), x.dtype),
            jax.ShapeDtypeStruct((copies, n_blocks, width, block_len), x.dtype),
        ),
        in_specs=[pl.BlockSpec(memory_space=pltpu.SMEM), vmem],
        out_specs=(vmem, vmem),
        name="pack",
    )(rows, x)


def pair_kernel(own_ref, partner_ref, out_ref):
    for n in range(out_ref.shape[0]):
        out_ref[n, 0] = own_ref[...]
        out_ref[n, 1] = partner_ref[...]


def pair(own, partner, copies):
    vmem = pl.BlockSpec(memory_space=pltpu.VMEM)
    return pl.pallas_call(
        pair_kernel,
        out_shape=jax.ShapeDtypeStruct((copies, 2) + own.shape, own.dtype),
        in_specs=[vmem, vmem],
        out_specs=vmem,
        name="pair",
    )(own, partner)


def tiles_kernel(here_ref, tile_rows_ref, tile_cols_ref, gain_ref, rows_ref, own_ref, got_z_ref, got_y_ref, got_zy_ref, w_ref, wd_ref, we_ref, wb_ref,
                 out_ref, acc, x_scr, d_scr, e_scr, w_scr, m_scr, lhs_scr, rep_scr, gain_scr):
    n_tiles, block_len, _ = w_ref.shape
    width = wd_ref.shape[0]
    n_blocks = rows_ref.shape[1] // width
    n_groups = width // GROUP
    n_chunks = block_len // CHUNK
    span = GROUP * CHUNK
    f32, bf16 = jnp.float32, jnp.bfloat16
    half = f32(0.5)
    acc[...] = jnp.zeros_like(acc)
    lane = lax.broadcasted_iota(jnp.int32, (block_len, n_chunks * span), 1)
    sub = lax.broadcasted_iota(jnp.int32, (block_len, n_chunks * span), 0)
    rep_scr[...] = (sub == lane // span * CHUNK + lane % CHUNK).astype(f32).astype(bf16)
    lane = lax.broadcasted_iota(jnp.int32, (GROUP, span), 1)
    sub = lax.broadcasted_iota(jnp.int32, (GROUP, span), 0)
    own = (lane // CHUNK == sub).astype(f32)

    lane = lax.broadcasted_iota(jnp.int32, (width, width), 1)
    sub = lax.broadcasted_iota(jnp.int32, (width, width), 0)
    column = jnp.sum(jnp.where(lane == sub, gain_ref[...], 0.0), axis=1, keepdims=True)
    gain_scr[...] = jnp.broadcast_to(column, gain_scr.shape)

    for t in range(n_tiles):
        at = slice(t * block_len, (t + 1) * block_len)
        owner, block = tile_rows_ref[t] // n_blocks, tile_rows_ref[t] % n_blocks
        panel = (owner // 4 * 2 + owner % 2) * 2 + ((owner // 2 % 2) ^ here_ref[2])
        x_scr[0, :, at] = rows_ref[panel, pl.ds(pl.multiple_of(block * width, width), width), :]
        owner = tile_cols_ref[t] // n_blocks
        source = ((owner // 4 % 2) ^ here_ref[0]) * 2 + ((owner % 2) ^ here_ref[1])
        place = (owner // 8 * 2 + owner // 2 % 2) * n_blocks + tile_cols_ref[t] % n_blocks
        for k, ref in enumerate((own_ref, got_y_ref, got_z_ref, got_zy_ref)):
            @pl.when(source == k)
            def _(ref=ref, at=at, t=t, k=k):
                x_scr[1, :, at] = ref[place if k == 0 else t]
    d_all = half * jnp.dot(wd_ref[...], x_scr[0], preferred_element_type=f32).astype(bf16).astype(f32)
    b_all = jnp.dot(wb_ref[...], x_scr[1], preferred_element_type=f32).astype(bf16)
    e_all = lax.dot_general(x_scr[1], we_ref[...], (((0,), (1,)), ((), ())), preferred_element_type=f32)
    e_all = (half * e_all.astype(bf16).astype(f32)).astype(bf16)
    for t in range(n_tiles):
        at = slice(t * block_len, (t + 1) * block_len)
        d_scr[t] = d_all[:, at]
        e_scr[t] = e_all[at, :]
        wt = w_ref[t].astype(f32).T
        m_scr[t] = (wt != 0).astype(f32).astype(bf16)
        w_scr[t] = half * wt
        for c in range(n_chunks):
            b_rep = jnp.dot(b_all[:, at], rep_scr[:, c * span:(c + 1) * span], preferred_element_type=f32)
            for g in range(n_groups):
                lhs_scr[t, c, g] = jnp.concatenate([b_rep[g * GROUP:(g + 1) * GROUP] * own, own], axis=0).astype(bf16)

    def tile(t, _):
        owner = tile_rows_ref[t] // n_blocks
        for c in range(n_chunks):
            at = slice(c * CHUNK, (c + 1) * CHUNK)
            w_c, m_c, e_c = w_scr[t, at, :], m_scr[t, at, :], e_scr[t, at, :]
            for g in range(n_groups):
                gates = []
                for k in range(GROUP):
                    f = g * GROUP + k
                    e_f = e_c[:, f:f + 1].astype(f32)
                    p = gain_scr[f:f + 1, :] * w_c + d_scr[t, f:f + 1, :] + e_f
                    gates.append((jnp.tanh(p) + 1.0).astype(bf16) * m_c)
                sums = jnp.dot(lhs_scr[t, c, g], jnp.concatenate(gates, axis=0), preferred_element_type=f32)
                acc[owner, g * GROUP:(g + 1) * GROUP, :] += sums[:GROUP]
                acc[owner, width + g * GROUP:width + (g + 1) * GROUP, :] += sums[GROUP:]
        return 0
    lax.fori_loop(0, n_tiles, tile, 0)
    out_ref[...] = (half * acc[...]).astype(out_ref.dtype)


def tile_sums(here, tile_rows, tile_cols, gain, rows, own, got_z, got_y, got_zy, w, wd, we, wb, n_owners):
    n_tiles, block_len, _ = w.shape
    width = wd.shape[0]
    smem = pl.BlockSpec(memory_space=pltpu.SMEM)
    vmem = pl.BlockSpec(memory_space=pltpu.VMEM)
    n_chunks, n_groups = block_len // CHUNK, width // GROUP
    return pl.pallas_call(
        tiles_kernel,
        out_shape=jax.ShapeDtypeStruct((n_owners, 2 * width, block_len), jnp.bfloat16),
        in_specs=[smem] * 3 + [vmem] * 10,
        out_specs=vmem,
        scratch_shapes=[
            pltpu.VMEM((n_owners, 2 * width, block_len), jnp.float32),
            pltpu.VMEM((2, width, n_tiles * block_len), jnp.bfloat16),
            pltpu.VMEM((n_tiles, width, block_len), jnp.float32),
            pltpu.VMEM((n_tiles, block_len, width), jnp.bfloat16),
            pltpu.VMEM((n_tiles, block_len, block_len), jnp.float32),
            pltpu.VMEM((n_tiles, block_len, block_len), jnp.bfloat16),
            pltpu.VMEM((n_tiles, n_chunks, n_groups, 2 * GROUP, GROUP * CHUNK), jnp.bfloat16),
            pltpu.VMEM((block_len, n_chunks * GROUP * CHUNK), jnp.bfloat16),
            pltpu.VMEM((width, block_len), jnp.float32),
        ],
        compiler_params=pltpu.CompilerParams(vmem_limit_bytes=32 * 1024 * 1024),
        name="tile_sums",
    )(here, tile_rows, tile_cols, gain, rows, own, got_z, got_y, got_zy, w, wd, we, wb)


def finish_kernel(here_ref, parts_ref, band_ref, x_ref, wa_ref, gain_ref, out_ref):
    width = wa_ref.shape[0]
    n_src, _, block_len = parts_ref.shape
    n_blocks = x_ref.shape[1] // block_len
    f32 = jnp.float32
    lane = lax.broadcasted_iota(jnp.int32, (width, width), 1)
    sub = lax.broadcasted_iota(jnp.int32, (width, width), 0)
    gain = jnp.sum(jnp.where(lane == sub, gain_ref[...], 0.0), axis=1, keepdims=True)
    first = (here_ref[3] * n_blocks).astype(f32)
    named = [band_ref[(s // 4 * 2 + s % 2) * 2 + ((s // 2 % 2) ^ here_ref[2])].astype(f32) for s in range(n_src)]
    for k in range(n_blocks):
        num = jnp.zeros((width, block_len), f32)
        den = jnp.zeros((width, block_len), f32)
        for s in range(n_src):
            hit = jnp.max((named[s] == first + float(k)).astype(f32), axis=0, keepdims=True)
            num += parts_ref[s, :width, :].astype(f32) * hit
            den += parts_ref[s, width:, :].astype(f32) * hit
        x = x_ref[:, k * block_len:(k + 1) * block_len]
        a = jnp.dot(wa_ref[...], x, preferred_element_type=f32)
        mixed = a + num / (den + 1e-6)
        center = mixed - jnp.mean(mixed, axis=0, keepdims=True)
        spread = jnp.mean(center * center, axis=0, keepdims=True)
        normed = center * lax.rsqrt(spread + 1e-5) * gain
        out_ref[:, k * block_len:(k + 1) * block_len] = (x.astype(f32) + jnp.maximum(normed, 0.0)).astype(jnp.bfloat16)


def finish(here, parts, rows, x, wa, gain):
    whole = lambda a: pl.BlockSpec(a.shape, lambda i: (0,) * a.ndim)
    n, depth, block_len = rows.shape
    return pl.pallas_call(
        finish_kernel,
        grid=(1,),
        out_shape=jax.ShapeDtypeStruct(x.shape, jnp.bfloat16),
        in_specs=[
            pl.BlockSpec(memory_space=pltpu.SMEM),
            whole(parts),
            pl.BlockSpec((n, BAND, block_len), lambda i: (0, depth // BAND - 1, 0)),
            whole(x), whole(wa), whole(gain),
        ],
        out_specs=whole(x),
        name="finish",
    )(here, parts, rows, x, wa, gain)


def flip(x, axes):
    last = 2 ** len(axes) - 1
    return lax.ppermute(x, axes, [(i, i ^ last) for i in range(last + 1)])


def local(x, edge_values, tile_rows, tile_cols, wa, wb, wd, we, edge_gain, ln_gain):
    width, shard = x.shape
    n_tiles, block_len = edge_values.shape[-3], edge_values.shape[-1]
    n_blocks = shard // block_len
    n_za, n_x = lax.axis_size("za"), lax.axis_size("x")
    rows, cols = tile_rows.reshape(-1), tile_cols.reshape(-1)
    tiles = edge_values.reshape(n_tiles, block_len, block_len)
    here = jnp.stack([lax.axis_index(a) for a in ("zb", "yb", "yhi", SRC)]).astype(jnp.int32)

    shard_rows, copies = pack(rows, x, block_len, n_za * 2)
    partner = flip(shard_rows, ("yhi",))
    held = lax.all_to_all(copies, ("za", "ya"), 0, 0).reshape(-1, width, block_len)
    cols_z = flip(cols, ("zb",))
    cols_y, cols_zy = flip(jnp.stack([cols, cols_z]), ("yb",))
    row_panel = lax.all_to_all(pair(shard_rows, partner, n_x * 2), ("x", "core"), 0, 0)
    row_panel = row_panel.reshape(n_x * 4, -1, block_len)

    def pick(names):
        owner = names // n_blocks
        place = (owner // 8 * 2 + owner // 2 % 2) * n_blocks + names % n_blocks
        return held.at[place].get(mode="promise_in_bounds")

    got_z = flip(pick(cols_z), ("zb",))
    got_y = flip(pick(cols_y), ("yb",))
    got_zy = flip(pick(cols_zy), ("zb", "yb"))

    parts = tile_sums(
        here, rows, cols, edge_gain[None], row_panel, held, got_z, got_y, got_zy, tiles, wd, we, wb, n_x * 4
    )
    parts = lax.all_to_all(parts, SRC, 0, 0)
    return finish(here, parts, row_panel, x, wa, ln_gain[None])


def solution(mesh):
    n_dst, n_src = mesh.devices.shape
    fine = Mesh(mesh.devices.reshape(n_dst // 8, 2, 2, 2, n_src // 4, 2, 2), AXES)
    in_specs = (
        P(None, AXES), P(DST, SRC, None, None, None), P(DST, SRC, None), P(DST, SRC, None),
        P(), P(), P(), P(), P(), P(),
    )
    return jax.shard_map(local, mesh=fine, in_specs=in_specs, out_specs=P(None, AXES), check_vma=False)
```

```python
import jax, jax.numpy as jnp
from jax import lax
from jax.sharding import Mesh, PartitionSpec as P
from jax.experimental import pallas as pl
from jax.experimental.pallas import tpu as pltpu

AXES = ("za", "zb", "ya", "yb", "x", "yhi", "core")
DST, SRC = AXES[:4], AXES[4:]
GROUP = 8
CHUNK = 128
BAND = 16


def pack_kernel(rows_ref, x_ref, shard_ref, spread_ref, both_ref):
    width, shard = x_ref.shape
    block_len = spread_ref.shape[3]
    n_tiles = rows_ref.shape[0]
    sub = lax.broadcasted_iota(jnp.int32, (BAND, block_len), 0)
    band = jnp.full((BAND, block_len), -1, jnp.int32)
    for t in range(n_tiles):
        band = jnp.where(sub == t, rows_ref[t], band)
    band = band.astype(jnp.float32).astype(shard_ref.dtype)
    for k in range(shard // block_len):
        block = x_ref[:, k * block_len:(k + 1) * block_len]
        at = slice(k * width, (k + 1) * width)
        shard_ref[at, :] = block
        for n in range(spread_ref.shape[0]):
            spread_ref[n, k] = block
        for n in range(both_ref.shape[0]):
            both_ref[n, 0, at, :] = block
    shard_ref[shard // block_len * width:, :] = band
    for n in range(both_ref.shape[0]):
        both_ref[n, 0, shard // block_len * width:, :] = band


def pack(rows, x, block_len, copies, pairs):
    width, shard = x.shape
    n_blocks = shard // block_len
    vmem = pl.BlockSpec(memory_space=pltpu.VMEM)
    return pl.pallas_call(
        pack_kernel,
        out_shape=(
            jax.ShapeDtypeStruct((n_blocks * width + BAND, block_len), x.dtype),
            jax.ShapeDtypeStruct((copies, n_blocks, width, block_len), x.dtype),
            jax.ShapeDtypeStruct((pairs, 2, n_blocks * width + BAND, block_len), x.dtype),
        ),
        in_specs=[pl.BlockSpec(memory_space=pltpu.SMEM), vmem],
        out_specs=(vmem, vmem, vmem),
        compiler_params=pltpu.CompilerParams(vmem_limit_bytes=4 * 1024 * 1024),
        name="pack",
    )(rows, x)


def pair_kernel(partner_ref, half_ref, out_ref, sem):
    del half_ref
    copies = [pltpu.make_async_copy(partner_ref, out_ref.at[n, 1], sem.at[n]) for n in range(out_ref.shape[0])]
    for copy in copies:
        copy.start()
    for copy in copies:
        copy.wait()


def pair(partner, half):
    anywhere = pl.BlockSpec(memory_space=pl.ANY)
    return pl.pallas_call(
        pair_kernel,
        out_shape=jax.ShapeDtypeStruct(half.shape, half.dtype),
        in_specs=[anywhere, anywhere],
        out_specs=anywhere,
        scratch_shapes=[pltpu.SemaphoreType.DMA((half.shape[0],))],
        input_output_aliases={1: 0},
        compiler_params=pltpu.CompilerParams(vmem_limit_bytes=2 * 1024 * 1024),
        name="pair",
    )(partner, half)


def tiles_kernel(here_ref, tile_rows_ref, tile_cols_ref, gain_ref, rows_ref, own_ref, got_z_ref, got_y_ref, got_zy_ref, w_ref, wd_ref, we_ref, wb_ref,
                 out_ref, acc, x_scr, d_scr, e_scr, w_scr, lhs_scr, rep_scr):
    n_tiles, block_len, _ = w_ref.shape
    width = wd_ref.shape[0]
    n_blocks = rows_ref.shape[1] // width
    n_groups = width // GROUP
    n_chunks = block_len // CHUNK
    span = GROUP * CHUNK
    f32, bf16 = jnp.float32, jnp.bfloat16
    half = f32(0.5)
    acc[...] = jnp.zeros_like(acc)
    lane = lax.broadcasted_iota(jnp.int32, (block_len, n_chunks * span), 1)
    sub = lax.broadcasted_iota(jnp.int32, (block_len, n_chunks * span), 0)
    rep_scr[...] = (sub == lane // span * CHUNK + lane % CHUNK).astype(f32).astype(bf16)
    lane = lax.broadcasted_iota(jnp.int32, (GROUP, span), 1)
    sub = lax.broadcasted_iota(jnp.int32, (GROUP, span), 0)
    own = (lane // CHUNK == sub).astype(f32)

    for t in range(n_tiles):
        at = slice(t * block_len, (t + 1) * block_len)
        owner, block = tile_rows_ref[t] // n_blocks, tile_rows_ref[t] % n_blocks
        panel = (owner // 4 * 2 + owner % 2) * 2 + ((owner // 2 % 2) ^ here_ref[2])
        x_scr[0, :, at] = rows_ref[panel, pl.ds(pl.multiple_of(block * width, width), width), :]
        owner = tile_cols_ref[t] // n_blocks
        source = ((owner // 4 % 2) ^ here_ref[0]) * 2 + ((owner % 2) ^ here_ref[1])
        place = (owner // 8 * 2 + owner // 2 % 2) * n_blocks + tile_cols_ref[t] % n_blocks
        for k, ref in enumerate((own_ref, got_y_ref, got_z_ref, got_zy_ref)):
            @pl.when(source == k)
            def _(ref=ref, at=at, t=t, k=k):
                x_scr[1, :, at] = ref[place if k == 0 else t]
    d_all = half * jnp.dot(wd_ref[...], x_scr[0], preferred_element_type=f32).astype(bf16).astype(f32)
    b_all = jnp.dot(wb_ref[...], x_scr[1], preferred_element_type=f32).astype(bf16)
    e_all = lax.dot_general(x_scr[1], we_ref[...], (((0,), (1,)), ((), ())), preferred_element_type=f32)
    e_all = (half * e_all.astype(bf16).astype(f32)).astype(bf16)
    for t in range(n_tiles):
        at = slice(t * block_len, (t + 1) * block_len)
        d_scr[t] = d_all[:, at]
        e_scr[t] = e_all[at, :]
        wt = w_ref[t].astype(f32).T
        w_scr[t, 0] = jnp.where(wt != 0, half * wt, -1e35)
        w_scr[t, 1] = jnp.where(wt != 0, -half * wt, -1e35)
        for c in range(n_chunks):
            b_rep = jnp.dot(b_all[:, at], rep_scr[:, c * span:(c + 1) * span], preferred_element_type=f32)
            for g in range(n_groups):
                lhs_scr[t, c, g] = jnp.concatenate([b_rep[g * GROUP:(g + 1) * GROUP] * own, own], axis=0).astype(bf16)

    def tile(t, _):
        owner = tile_rows_ref[t] // n_blocks
        for c in range(n_chunks):
            at = slice(c * CHUNK, (c + 1) * CHUNK)
            e_c = e_scr[t, at, :]
            for g in range(n_groups):
                gates = []
                for k in range(GROUP):
                    f = g * GROUP + k
                    gain = gain_ref[f]
                    w_f = w_scr[t, (gain < 0).astype(jnp.int32), at, :]
                    p = jnp.maximum(jnp.abs(gain), 1e-30) * w_f + d_scr[t, f:f + 1, :] + e_c[:, f:f + 1].astype(f32)
                    gates.append((jnp.tanh(p) + 1.0).astype(bf16))
                sums = jnp.dot(lhs_scr[t, c, g], jnp.concatenate(gates, axis=0), preferred_element_type=f32)
                acc[owner, g * GROUP:(g + 1) * GROUP, :] += sums[:GROUP]
                acc[owner, width + g * GROUP:width + (g + 1) * GROUP, :] += sums[GROUP:]
        return 0
    lax.fori_loop(0, n_tiles, tile, 0)
    out_ref[...] = (half * acc[...]).astype(out_ref.dtype)


def tile_sums(here, tile_rows, tile_cols, gain, rows, own, got_z, got_y, got_zy, w, wd, we, wb, n_owners):
    n_tiles, block_len, _ = w.shape
    width = wd.shape[0]
    smem = pl.BlockSpec(memory_space=pltpu.SMEM)
    vmem = pl.BlockSpec(memory_space=pltpu.VMEM)
    n_chunks, n_groups = block_len // CHUNK, width // GROUP
    return pl.pallas_call(
        tiles_kernel,
        out_shape=jax.ShapeDtypeStruct((n_owners, 2 * width, block_len), jnp.bfloat16),
        in_specs=[smem] * 4 + [vmem] * 9,
        out_specs=vmem,
        scratch_shapes=[
            pltpu.VMEM((n_owners, 2 * width, block_len), jnp.float32),
            pltpu.VMEM((2, width, n_tiles * block_len), jnp.bfloat16),
            pltpu.VMEM((n_tiles, width, block_len), jnp.float32),
            pltpu.VMEM((n_tiles, block_len, width), jnp.bfloat16),
            pltpu.VMEM((n_tiles, 2, block_len, block_len), jnp.float32),
            pltpu.VMEM((n_tiles, n_chunks, n_groups, 2 * GROUP, GROUP * CHUNK), jnp.bfloat16),
            pltpu.VMEM((block_len, n_chunks * GROUP * CHUNK), jnp.bfloat16),
        ],
        compiler_params=pltpu.CompilerParams(vmem_limit_bytes=32 * 1024 * 1024),
        name="tile_sums",
    )(here, tile_rows, tile_cols, gain, rows, own, got_z, got_y, got_zy, w, wd, we, wb)


def finish_kernel(here_ref, parts_ref, band_ref, x_ref, wa_ref, gain_ref, out_ref):
    width = wa_ref.shape[0]
    n_src, _, block_len = parts_ref.shape
    n_blocks = x_ref.shape[1] // block_len
    f32 = jnp.float32
    lane = lax.broadcasted_iota(jnp.int32, (width, width), 1)
    sub = lax.broadcasted_iota(jnp.int32, (width, width), 0)
    gain = jnp.sum(jnp.where(lane == sub, gain_ref[...], 0.0), axis=1, keepdims=True)
    first = (here_ref[3] * n_blocks).astype(f32)
    named = [band_ref[(s // 4 * 2 + s % 2) * 2 + ((s // 2 % 2) ^ here_ref[2])].astype(f32) for s in range(n_src)]
    for k in range(n_blocks):
        num = jnp.zeros((width, block_len), f32)
        den = jnp.zeros((width, block_len), f32)
        for s in range(n_src):
            hit = jnp.max((named[s] == first + float(k)).astype(f32), axis=0, keepdims=True)
            num += parts_ref[s, :width, :].astype(f32) * hit
            den += parts_ref[s, width:, :].astype(f32) * hit
        x = x_ref[:, k * block_len:(k + 1) * block_len]
        a = jnp.dot(wa_ref[...], x, preferred_element_type=f32)
        mixed = a + num / (den + 1e-6)
        center = mixed - jnp.mean(mixed, axis=0, keepdims=True)
        spread = jnp.mean(center * center, axis=0, keepdims=True)
        normed = center * lax.rsqrt(spread + 1e-5) * gain
        out_ref[:, k * block_len:(k + 1) * block_len] = (x.astype(f32) + jnp.maximum(normed, 0.0)).astype(jnp.bfloat16)


def finish(here, parts, rows, x, wa, gain):
    whole = lambda a: pl.BlockSpec(a.shape, lambda i: (0,) * a.ndim)
    n, depth, block_len = rows.shape
    return pl.pallas_call(
        finish_kernel,
        grid=(1,),
        out_shape=jax.ShapeDtypeStruct(x.shape, jnp.bfloat16),
        in_specs=[
            pl.BlockSpec(memory_space=pltpu.SMEM),
            whole(parts),
            pl.BlockSpec((n, BAND, block_len), lambda i: (0, depth // BAND - 1, 0)),
            whole(x), whole(wa), whole(gain),
        ],
        out_specs=whole(x),
        compiler_params=pltpu.CompilerParams(vmem_limit_bytes=8 * 1024 * 1024),
        name="finish",
    )(here, parts, rows, x, wa, gain)


def flip(x, axes):
    last = 2 ** len(axes) - 1
    return lax.ppermute(x, axes, [(i, i ^ last) for i in range(last + 1)])


def local(x, edge_values, tile_rows, tile_cols, wa, wb, wd, we, edge_gain, ln_gain):
    width, shard = x.shape
    n_tiles, block_len = edge_values.shape[-3], edge_values.shape[-1]
    n_blocks = shard // block_len
    n_za, n_x = lax.axis_size("za"), lax.axis_size("x")
    rows, cols = tile_rows.reshape(-1), tile_cols.reshape(-1)
    tiles = edge_values.reshape(n_tiles, block_len, block_len)
    here = jnp.stack([lax.axis_index(a) for a in ("zb", "yb", "yhi", SRC)]).astype(jnp.int32)

    shard_rows, copies, both = pack(rows, x, block_len, n_za * 2, n_x * 2)
    partner = flip(shard_rows, ("yhi",))
    held = lax.all_to_all(copies, ("za", "ya"), 0, 0).reshape(-1, width, block_len)
    cols_z = flip(cols, ("zb",))
    cols_y = flip(cols, ("yb",))
    cols_zy = flip(cols, ("zb", "yb"))
    row_panel = lax.all_to_all(pair(partner, both), ("x", "core"), 0, 0)
    row_panel = row_panel.reshape(n_x * 4, -1, block_len)

    def pick(names):
        owner = names // n_blocks
        place = (owner // 8 * 2 + owner // 2 % 2) * n_blocks + names % n_blocks
        return held.at[place].get(mode="promise_in_bounds")

    got_z = flip(pick(cols_z), ("zb",))
    got_y = flip(pick(cols_y), ("yb",))
    got_zy = flip(pick(cols_zy), ("zb", "yb"))

    parts = tile_sums(
        here, rows, cols, edge_gain, row_panel, held, got_z, got_y, got_zy, tiles, wd, we, wb, n_x * 4
    )
    parts = lax.all_to_all(parts, SRC, 0, 0)
    return finish(here, parts, row_panel, x, wa, ln_gain[None])


def solution(mesh):
    n_dst, n_src = mesh.devices.shape
    fine = Mesh(mesh.devices.reshape(n_dst // 8, 2, 2, 2, n_src // 4, 2, 2), AXES)
    in_specs = (
        P(None, AXES), P(DST, SRC, None, None, None), P(DST, SRC, None), P(DST, SRC, None),
        P(), P(), P(), P(), P(), P(),
    )
    return jax.shard_map(local, mesh=fine, in_specs=in_specs, out_specs=P(None, AXES), check_vma=False)
```

```python
import jax, jax.numpy as jnp
from jax import lax
from jax.sharding import Mesh, PartitionSpec as P
from jax.experimental import pallas as pl
from jax.experimental.pallas import tpu as pltpu

AXES = ("za", "zb", "ya", "yb", "x", "yhi", "core")
DST, SRC = AXES[:4], AXES[4:]
GROUP = 8
CHUNK = 128
BAND = 16


def pack_kernel(rows_ref, x_ref, shard_ref, spread_ref, both_ref):
    width, shard = x_ref.shape
    block_len = spread_ref.shape[3]
    n_tiles = rows_ref.shape[0]
    sub = lax.broadcasted_iota(jnp.int32, (BAND, block_len), 0)
    band = jnp.full((BAND, block_len), -1, jnp.int32)
    for t in range(n_tiles):
        band = jnp.where(sub == t, rows_ref[t], band)
    band = band.astype(jnp.float32).astype(shard_ref.dtype)
    for k in range(shard // block_len):
        block = x_ref[:, k * block_len:(k + 1) * block_len]
        at = slice(k * width, (k + 1) * width)
        shard_ref[at, :] = block
        for n in range(spread_ref.shape[0]):
            spread_ref[n, k] = block
        for n in range(both_ref.shape[0]):
            both_ref[n, 0, at, :] = block
    shard_ref[shard // block_len * width:, :] = band
    for n in range(both_ref.shape[0]):
        both_ref[n, 0, shard // block_len * width:, :] = band


def pack(rows, x, block_len, copies, pairs):
    width, shard = x.shape
    n_blocks = shard // block_len
    vmem = pl.BlockSpec(memory_space=pltpu.VMEM)
    return pl.pallas_call(
        pack_kernel,
        out_shape=(
            jax.ShapeDtypeStruct((n_blocks * width + BAND, block_len), x.dtype),
            jax.ShapeDtypeStruct((copies, n_blocks, width, block_len), x.dtype),
            jax.ShapeDtypeStruct((pairs, 2, n_blocks * width + BAND, block_len), x.dtype),
        ),
        in_specs=[pl.BlockSpec(memory_space=pltpu.SMEM), vmem],
        out_specs=(vmem, vmem, vmem),
        name="pack",
    )(rows, x)


def pair_kernel(partner_ref, half_ref, out_ref, sem):
    del half_ref
    copies = [pltpu.make_async_copy(partner_ref, out_ref.at[n, 1], sem.at[n]) for n in range(out_ref.shape[0])]
    for copy in copies:
        copy.start()
    for copy in copies:
        copy.wait()


def pair(partner, half):
    anywhere = pl.BlockSpec(memory_space=pl.ANY)
    return pl.pallas_call(
        pair_kernel,
        out_shape=jax.ShapeDtypeStruct(half.shape, half.dtype),
        in_specs=[pl.BlockSpec(memory_space=pltpu.VMEM), anywhere],
        out_specs=anywhere,
        scratch_shapes=[pltpu.SemaphoreType.DMA((half.shape[0],))],
        input_output_aliases={1: 0},
        name="pair",
    )(partner, half)


def tiles_kernel(here_ref, tile_rows_ref, tile_cols_ref, gain_ref, rows_ref, own_ref, got_z_ref, got_y_ref, got_zy_ref, w_ref, wd_ref, we_ref, wb_ref,
                 out_ref, acc, x_scr, d_scr, e_scr, w_scr, lhs_scr, rep_scr):
    n_tiles, block_len, _ = w_ref.shape
    width = wd_ref.shape[0]
    n_blocks = rows_ref.shape[1] // width
    n_groups = width // GROUP
    n_chunks = block_len // CHUNK
    span = GROUP * CHUNK
    f32, bf16 = jnp.float32, jnp.bfloat16
    half = f32(0.5)
    acc[...] = jnp.zeros_like(acc)
    lane = lax.broadcasted_iota(jnp.int32, (block_len, n_chunks * span), 1)
    sub = lax.broadcasted_iota(jnp.int32, (block_len, n_chunks * span), 0)
    rep_scr[...] = (sub == lane // span * CHUNK + lane % CHUNK).astype(f32).astype(bf16)
    lane = lax.broadcasted_iota(jnp.int32, (GROUP, span), 1)
    sub = lax.broadcasted_iota(jnp.int32, (GROUP, span), 0)
    own = (lane // CHUNK == sub).astype(f32)

    for t in range(n_tiles):
        at = slice(t * block_len, (t + 1) * block_len)
        owner, block = tile_rows_ref[t] // n_blocks, tile_rows_ref[t] % n_blocks
        panel = (owner // 4 * 2 + owner % 2) * 2 + ((owner // 2 % 2) ^ here_ref[2])
        x_scr[0, :, at] = rows_ref[panel, pl.ds(pl.multiple_of(block * width, width), width), :]
        owner = tile_cols_ref[t] // n_blocks
        source = ((owner // 4 % 2) ^ here_ref[0]) * 2 + ((owner % 2) ^ here_ref[1])
        place = (owner // 8 * 2 + owner // 2 % 2) * n_blocks + tile_cols_ref[t] % n_blocks
        for k, ref in enumerate((own_ref, got_y_ref, got_z_ref, got_zy_ref)):
            @pl.when(source == k)
            def _(ref=ref, at=at, t=t, k=k):
                x_scr[1, :, at] = ref[place if k == 0 else t]
    d_all = half * jnp.dot(wd_ref[...], x_scr[0], preferred_element_type=f32).astype(bf16).astype(f32)
    b_all = jnp.dot(wb_ref[...], x_scr[1], preferred_element_type=f32).astype(bf16)
    e_all = lax.dot_general(x_scr[1], we_ref[...], (((0,), (1,)), ((), ())), preferred_element_type=f32)
    e_all = (half * e_all.astype(bf16).astype(f32)).astype(bf16)
    for t in range(n_tiles):
        at = slice(t * block_len, (t + 1) * block_len)
        d_scr[t] = d_all[:, at]
        e_scr[t] = e_all[at, :]
        wt = w_ref[t].astype(f32).T
        w_scr[t, 0] = jnp.where(wt != 0, half * wt, -1e35)
        w_scr[t, 1] = jnp.where(wt != 0, -half * wt, -1e35)
        for c in range(n_chunks):
            b_rep = jnp.dot(b_all[:, at], rep_scr[:, c * span:(c + 1) * span], preferred_element_type=f32)
            for g in range(n_groups):
                lhs_scr[t, c, g] = jnp.concatenate([b_rep[g * GROUP:(g + 1) * GROUP] * own, own], axis=0).astype(bf16)

    def tile(t, _):
        owner = tile_rows_ref[t] // n_blocks
        for c in range(n_chunks):
            at = slice(c * CHUNK, (c + 1) * CHUNK)
            e_c = e_scr[t, at, :]
            for g in range(n_groups):
                gates = []
                for k in range(GROUP):
                    f = g * GROUP + k
                    gain = gain_ref[f]
                    w_f = w_scr[t, (gain < 0).astype(jnp.int32), at, :]
                    p = jnp.maximum(jnp.abs(gain), 1e-30) * w_f + d_scr[t, f:f + 1, :] + e_c[:, f:f + 1].astype(f32)
                    gates.append((jnp.tanh(p) + 1.0).astype(bf16))
                sums = jnp.dot(lhs_scr[t, c, g], jnp.concatenate(gates, axis=0), preferred_element_type=f32)
                acc[owner, g * GROUP:(g + 1) * GROUP, :] += sums[:GROUP]
                acc[owner, width + g * GROUP:width + (g + 1) * GROUP, :] += sums[GROUP:]
        return 0
    lax.fori_loop(0, n_tiles, tile, 0)
    out_ref[...] = (half * acc[...]).astype(out_ref.dtype)


def tile_sums(here, tile_rows, tile_cols, gain, rows, own, got_z, got_y, got_zy, w, wd, we, wb, n_owners):
    n_tiles, block_len, _ = w.shape
    width = wd.shape[0]
    smem = pl.BlockSpec(memory_space=pltpu.SMEM)
    vmem = pl.BlockSpec(memory_space=pltpu.VMEM)
    n_chunks, n_groups = block_len // CHUNK, width // GROUP
    return pl.pallas_call(
        tiles_kernel,
        out_shape=jax.ShapeDtypeStruct((n_owners, 2 * width, block_len), jnp.bfloat16),
        in_specs=[smem] * 4 + [vmem] * 9,
        out_specs=vmem,
        scratch_shapes=[
            pltpu.VMEM((n_owners, 2 * width, block_len), jnp.float32),
            pltpu.VMEM((2, width, n_tiles * block_len), jnp.bfloat16),
            pltpu.VMEM((n_tiles, width, block_len), jnp.float32),
            pltpu.VMEM((n_tiles, block_len, width), jnp.bfloat16),
            pltpu.VMEM((n_tiles, 2, block_len, block_len), jnp.float32),
            pltpu.VMEM((n_tiles, n_chunks, n_groups, 2 * GROUP, GROUP * CHUNK), jnp.bfloat16),
            pltpu.VMEM((block_len, n_chunks * GROUP * CHUNK), jnp.bfloat16),
        ],
        compiler_params=pltpu.CompilerParams(vmem_limit_bytes=32 * 1024 * 1024),
        name="tile_sums",
    )(here, tile_rows, tile_cols, gain, rows, own, got_z, got_y, got_zy, w, wd, we, wb)


def finish_kernel(here_ref, parts_ref, band_ref, x_ref, wa_ref, gain_ref, out_ref):
    width = wa_ref.shape[0]
    n_src, _, block_len = parts_ref.shape
    n_blocks = x_ref.shape[1] // block_len
    f32 = jnp.float32
    lane = lax.broadcasted_iota(jnp.int32, (width, width), 1)
    sub = lax.broadcasted_iota(jnp.int32, (width, width), 0)
    gain = jnp.sum(jnp.where(lane == sub, gain_ref[...], 0.0), axis=1, keepdims=True)
    first = (here_ref[3] * n_blocks).astype(f32)
    named = [band_ref[(s // 4 * 2 + s % 2) * 2 + ((s // 2 % 2) ^ here_ref[2])].astype(f32) for s in range(n_src)]
    for k in range(n_blocks):
        num = jnp.zeros((width, block_len), f32)
        den = jnp.zeros((width, block_len), f32)
        for s in range(n_src):
            hit = jnp.max((named[s] == first + float(k)).astype(f32), axis=0, keepdims=True)
            num += parts_ref[s, :width, :].astype(f32) * hit
            den += parts_ref[s, width:, :].astype(f32) * hit
        x = x_ref[:, k * block_len:(k + 1) * block_len]
        a = jnp.dot(wa_ref[...], x, preferred_element_type=f32)
        mixed = a + num / (den + 1e-6)
        center = mixed - jnp.mean(mixed, axis=0, keepdims=True)
        spread = jnp.mean(center * center, axis=0, keepdims=True)
        normed = center * lax.rsqrt(spread + 1e-5) * gain
        out_ref[:, k * block_len:(k + 1) * block_len] = (x.astype(f32) + jnp.maximum(normed, 0.0)).astype(jnp.bfloat16)


def finish(here, parts, rows, x, wa, gain):
    whole = lambda a: pl.BlockSpec(a.shape, lambda i: (0,) * a.ndim)
    n, depth, block_len = rows.shape
    return pl.pallas_call(
        finish_kernel,
        grid=(1,),
        out_shape=jax.ShapeDtypeStruct(x.shape, jnp.bfloat16),
        in_specs=[
            pl.BlockSpec(memory_space=pltpu.SMEM),
            whole(parts),
            pl.BlockSpec((n, BAND, block_len), lambda i: (0, depth // BAND - 1, 0)),
            whole(x), whole(wa), whole(gain),
        ],
        out_specs=whole(x),
        name="finish",
    )(here, parts, rows, x, wa, gain)


def flip(x, axes):
    last = 2 ** len(axes) - 1
    return lax.ppermute(x, axes, [(i, i ^ last) for i in range(last + 1)])


def local(x, edge_values, tile_rows, tile_cols, wa, wb, wd, we, edge_gain, ln_gain):
    width, shard = x.shape
    n_tiles, block_len = edge_values.shape[-3], edge_values.shape[-1]
    n_blocks = shard // block_len
    n_za, n_x = lax.axis_size("za"), lax.axis_size("x")
    rows, cols = tile_rows.reshape(-1), tile_cols.reshape(-1)
    tiles = edge_values.reshape(n_tiles, block_len, block_len)
    here = jnp.stack([lax.axis_index(a) for a in ("zb", "yb", "yhi", SRC)]).astype(jnp.int32)

    shard_rows, copies, both = pack(rows, x, block_len, n_za * 2, n_x * 2)
    partner = flip(shard_rows, ("yhi",))
    held = lax.all_to_all(copies, ("za", "ya"), 0, 0).reshape(-1, width, block_len)
    asked, _ = lax.optimization_barrier((cols, shard_rows))
    cols_z = flip(asked, ("zb",))
    cols_y, cols_zy = flip(jnp.stack([asked, cols_z]), ("yb",))
    row_panel = lax.all_to_all(pair(partner, both), ("x", "core"), 0, 0)
    row_panel = row_panel.reshape(n_x * 4, -1, block_len)

    def pick(names):
        owner = names // n_blocks
        place = (owner // 8 * 2 + owner // 2 % 2) * n_blocks + names % n_blocks
        return held.at[place].get(mode="promise_in_bounds")

    got_z = flip(pick(cols_z), ("zb",))
    got_y = flip(pick(cols_y), ("yb",))
    got_zy = flip(pick(cols_zy), ("zb", "yb"))

    parts = tile_sums(
        here, rows, cols, edge_gain, row_panel, held, got_z, got_y, got_zy, tiles, wd, we, wb, n_x * 4
    )
    parts = lax.all_to_all(parts, SRC, 0, 0)
    return finish(here, parts, row_panel, x, wa, ln_gain[None])


def solution(mesh):
    n_dst, n_src = mesh.devices.shape
    fine = Mesh(mesh.devices.reshape(n_dst // 8, 2, 2, 2, n_src // 4, 2, 2), AXES)
    in_specs = (
        P(None, AXES), P(DST, SRC, None, None, None), P(DST, SRC, None), P(DST, SRC, None),
        P(), P(), P(), P(), P(), P(),
    )
    return jax.shard_map(local, mesh=fine, in_specs=in_specs, out_specs=P(None, AXES), check_vma=False)
```

```python
import functools

import jax, jax.numpy as jnp
from jax import lax
from jax.sharding import Mesh, PartitionSpec as P
from jax.experimental import pallas as pl
from jax.experimental.pallas import tpu as pltpu

AXES = ("za", "zb", "ya", "yb", "x", "yhi", "core")
DST, SRC = AXES[:4], AXES[4:]
GROUP = 8
CHUNK = 128
BAND = 16


def pack_kernel(rows_ref, x_ref, shard_ref, spread_ref, both_ref):
    width, shard = x_ref.shape
    block_len = spread_ref.shape[3]
    n_tiles = rows_ref.shape[0]
    sub = lax.broadcasted_iota(jnp.int32, (BAND, block_len), 0)
    band = jnp.full((BAND, block_len), -1, jnp.int32)
    for t in range(n_tiles):
        band = jnp.where(sub == t, rows_ref[t], band)
    band = band.astype(jnp.float32).astype(shard_ref.dtype)
    for k in range(shard // block_len):
        block = x_ref[:, k * block_len:(k + 1) * block_len]
        at = slice(k * width, (k + 1) * width)
        shard_ref[at, :] = block
        for n in range(spread_ref.shape[0]):
            spread_ref[n, k] = block
        for n in range(both_ref.shape[0]):
            both_ref[n, 0, at, :] = block
    shard_ref[shard // block_len * width:, :] = band
    for n in range(both_ref.shape[0]):
        both_ref[n, 0, shard // block_len * width:, :] = band


def pack(rows, x, block_len, copies, pairs):
    width, shard = x.shape
    n_blocks = shard // block_len
    vmem = pl.BlockSpec(memory_space=pltpu.VMEM)
    return pl.pallas_call(
        pack_kernel,
        out_shape=(
            jax.ShapeDtypeStruct((n_blocks * width + BAND, block_len), x.dtype),
            jax.ShapeDtypeStruct((copies, n_blocks, width, block_len), x.dtype),
            jax.ShapeDtypeStruct((pairs, 2, n_blocks * width + BAND, block_len), x.dtype),
        ),
        in_specs=[pl.BlockSpec(memory_space=pltpu.SMEM), vmem],
        out_specs=(vmem, vmem, vmem),
        name="pack",
    )(rows, x)


def pair_kernel(partner_ref, half_ref, out_ref, sem):
    del half_ref
    copies = [pltpu.make_async_copy(partner_ref, out_ref.at[n, 1], sem.at[n]) for n in range(out_ref.shape[0])]
    for copy in copies:
        copy.start()
    for copy in copies:
        copy.wait()


def pair(partner, half):
    anywhere = pl.BlockSpec(memory_space=pl.ANY)
    return pl.pallas_call(
        pair_kernel,
        out_shape=jax.ShapeDtypeStruct(half.shape, half.dtype),
        in_specs=[pl.BlockSpec(memory_space=pltpu.VMEM), anywhere],
        out_specs=anywhere,
        scratch_shapes=[pltpu.SemaphoreType.DMA((half.shape[0],))],
        input_output_aliases={1: 0},
        name="pair",
    )(partner, half)


def tiles_kernel(here_ref, tile_rows_ref, tile_cols_ref, gain_ref, rows_ref, own_ref, got_z_ref, got_y_ref, got_zy_ref, w_ref, wd_ref, we_ref, wb_ref,
                 out_ref, acc, x_scr, d_scr, e_scr, w_scr, lhs_scr, rep_scr):
    n_tiles, block_len, _ = w_ref.shape
    width = wd_ref.shape[0]
    n_blocks = rows_ref.shape[1] // width
    n_groups = width // GROUP
    n_chunks = block_len // CHUNK
    span = GROUP * CHUNK
    f32, bf16 = jnp.float32, jnp.bfloat16
    half = f32(0.5)
    acc[...] = jnp.zeros_like(acc)
    lane = lax.broadcasted_iota(jnp.int32, (block_len, n_chunks * span), 1)
    sub = lax.broadcasted_iota(jnp.int32, (block_len, n_chunks * span), 0)
    rep_scr[...] = (sub == lane // span * CHUNK + lane % CHUNK).astype(f32).astype(bf16)
    lane = lax.broadcasted_iota(jnp.int32, (GROUP, span), 1)
    sub = lax.broadcasted_iota(jnp.int32, (GROUP, span), 0)
    own = (lane // CHUNK == sub).astype(f32)

    for t in range(n_tiles):
        at = slice(t * block_len, (t + 1) * block_len)
        owner, block = tile_rows_ref[t] // n_blocks, tile_rows_ref[t] % n_blocks
        panel = (owner // 4 * 2 + owner % 2) * 2 + ((owner // 2 % 2) ^ here_ref[2])
        x_scr[0, :, at] = rows_ref[panel, pl.ds(pl.multiple_of(block * width, width), width), :]
        owner = tile_cols_ref[t] // n_blocks
        source = ((owner // 4 % 2) ^ here_ref[0]) * 2 + ((owner % 2) ^ here_ref[1])
        place = (owner // 8 * 2 + owner // 2 % 2) * n_blocks + tile_cols_ref[t] % n_blocks
        for k, ref in enumerate((own_ref, got_y_ref, got_z_ref, got_zy_ref)):
            @pl.when(source == k)
            def _(ref=ref, at=at, t=t, k=k):
                x_scr[1, :, at] = ref[place if k == 0 else t]
    d_all = half * jnp.dot(wd_ref[...], x_scr[0], preferred_element_type=f32).astype(bf16).astype(f32)
    b_all = jnp.dot(wb_ref[...], x_scr[1], preferred_element_type=f32).astype(bf16)
    e_all = lax.dot_general(x_scr[1], we_ref[...], (((0,), (1,)), ((), ())), preferred_element_type=f32)
    e_all = (half * e_all.astype(bf16).astype(f32)).astype(bf16)
    for t in range(n_tiles):
        at = slice(t * block_len, (t + 1) * block_len)
        d_scr[t] = d_all[:, at]
        e_scr[t] = e_all[at, :]
        wt = w_ref[t].astype(f32).T
        w_scr[t, 0] = jnp.where(wt != 0, half * wt, -1e35)
        w_scr[t, 1] = jnp.where(wt != 0, -half * wt, -1e35)
        for c in range(n_chunks):
            b_rep = jnp.dot(b_all[:, at], rep_scr[:, c * span:(c + 1) * span], preferred_element_type=f32)
            for g in range(n_groups):
                lhs_scr[t, c, g] = jnp.concatenate([b_rep[g * GROUP:(g + 1) * GROUP] * own, own], axis=0).astype(bf16)

    def tile(t, _):
        owner = tile_rows_ref[t] // n_blocks
        slot = (owner // 4 * 2 + owner % 2) * 2 + ((owner // 2 % 2) ^ here_ref[2])
        for c in range(n_chunks):
            at = slice(c * CHUNK, (c + 1) * CHUNK)
            e_c = e_scr[t, at, :]
            for g in range(n_groups):
                gates = []
                for k in range(GROUP):
                    f = g * GROUP + k
                    gain = gain_ref[f]
                    w_f = w_scr[t, (gain < 0).astype(jnp.int32), at, :]
                    p = jnp.maximum(jnp.abs(gain), 1e-30) * w_f + d_scr[t, f:f + 1, :] + e_c[:, f:f + 1].astype(f32)
                    gates.append((jnp.tanh(p) + 1.0).astype(bf16))
                sums = jnp.dot(lhs_scr[t, c, g], jnp.concatenate(gates, axis=0), preferred_element_type=f32)
                acc[slot, g * GROUP:(g + 1) * GROUP, :] += sums[:GROUP]
                acc[slot, width + g * GROUP:width + (g + 1) * GROUP, :] += sums[GROUP:]
        return 0
    lax.fori_loop(0, n_tiles, tile, 0)
    out_ref[...] = (half * acc[...]).astype(out_ref.dtype)


def tile_sums(here, tile_rows, tile_cols, gain, rows, own, got_z, got_y, got_zy, w, wd, we, wb, n_owners):
    n_tiles, block_len, _ = w.shape
    width = wd.shape[0]
    smem = pl.BlockSpec(memory_space=pltpu.SMEM)
    vmem = pl.BlockSpec(memory_space=pltpu.VMEM)
    n_chunks, n_groups = block_len // CHUNK, width // GROUP
    return pl.pallas_call(
        tiles_kernel,
        out_shape=jax.ShapeDtypeStruct((n_owners, 2 * width, block_len), jnp.bfloat16),
        in_specs=[smem] * 4 + [vmem] * 9,
        out_specs=vmem,
        scratch_shapes=[
            pltpu.VMEM((n_owners, 2 * width, block_len), jnp.float32),
            pltpu.VMEM((2, width, n_tiles * block_len), jnp.bfloat16),
            pltpu.VMEM((n_tiles, width, block_len), jnp.float32),
            pltpu.VMEM((n_tiles, block_len, width), jnp.bfloat16),
            pltpu.VMEM((n_tiles, 2, block_len, block_len), jnp.float32),
            pltpu.VMEM((n_tiles, n_chunks, n_groups, 2 * GROUP, GROUP * CHUNK), jnp.bfloat16),
            pltpu.VMEM((block_len, n_chunks * GROUP * CHUNK), jnp.bfloat16),
        ],
        compiler_params=pltpu.CompilerParams(vmem_limit_bytes=32 * 1024 * 1024),
        name="tile_sums",
    )(here, tile_rows, tile_cols, gain, rows, own, got_z, got_y, got_zy, w, wd, we, wb)


def sums_kernel(flipped, here_ref, parts_ref, band_ref, out_ref):
    n_senders = parts_ref.shape[0]
    n_blocks = out_ref.shape[0]
    f32 = jnp.float32
    first = ((here_ref[3] ^ flipped) * n_blocks).astype(f32)
    named = [band_ref[s, 0].astype(f32) for s in range(n_senders)]
    for k in range(n_blocks):
        total = jnp.zeros(out_ref.shape[1:], f32)
        for s in range(n_senders):
            hit = jnp.max((named[s] == first + float(k)).astype(f32), axis=0, keepdims=True)
            total += parts_ref[s, 0].astype(f32) * hit
        out_ref[k] = total.astype(out_ref.dtype)


def own_kernel(here_ref, parts_ref, band_ref, x_ref, wa_ref, gain_ref, out_ref, proj_ref, gains_ref):
    width = wa_ref.shape[0]
    lane = lax.broadcasted_iota(jnp.int32, (width, width), 1)
    sub = lax.broadcasted_iota(jnp.int32, (width, width), 0)
    gain = jnp.sum(jnp.where(lane == sub, gain_ref[...], 0.0), axis=1, keepdims=True)
    gains_ref[...] = jnp.broadcast_to(gain, gains_ref.shape)
    proj_ref[...] = jnp.dot(wa_ref[...], x_ref[...], preferred_element_type=jnp.float32)
    sums_kernel(0, here_ref, parts_ref, band_ref, out_ref)


def whole(shape):
    return pl.BlockSpec(shape, lambda i: (0,) * len(shape))


def sums_specs(parts, panel, side):
    n, _, depth, block_len = parts.shape
    return [
        pl.BlockSpec(memory_space=pltpu.SMEM),
        pl.BlockSpec((n, 1, depth, block_len), lambda i: (0, side, 0, 0)),
        pl.BlockSpec((n, 1, BAND, block_len), lambda i: (0, 0, panel.shape[2] // BAND - 1, 0)),
    ]


GRANT = pltpu.CompilerParams(vmem_limit_bytes=4 * 1024 * 1024)


def far_sums(here, parts, panel, n_blocks):
    shape = (n_blocks,) + parts.shape[2:]
    return pl.pallas_call(
        functools.partial(sums_kernel, 2),
        grid=(1,),
        out_shape=jax.ShapeDtypeStruct(shape, jnp.bfloat16),
        in_specs=sums_specs(parts, panel, 1),
        out_specs=whole(shape),
        compiler_params=GRANT,
        name="far_sums",
    )(here, parts, panel)


def own_sums(here, parts, panel, x, wa, gain):
    width, shard = x.shape
    shape = (shard // parts.shape[3],) + parts.shape[2:]
    shapes = (shape, x.shape, (width, parts.shape[3]))
    return pl.pallas_call(
        own_kernel,
        grid=(1,),
        out_shape=tuple(jax.ShapeDtypeStruct(a, jnp.float32) for a in shapes),
        in_specs=sums_specs(parts, panel, 0) + [whole(x.shape), whole(wa.shape), whole(gain.shape)],
        out_specs=tuple(whole(a) for a in shapes),
        compiler_params=GRANT,
        name="own_sums",
    )(here, parts, panel, x, wa, gain)


def finish_kernel(got_ref, own_ref, proj_ref, gains_ref, x_ref, out_ref):
    width = x_ref.shape[0]
    n_blocks, _, block_len = own_ref.shape
    f32 = jnp.float32
    for k in range(n_blocks):
        at = slice(k * block_len, (k + 1) * block_len)
        num = own_ref[k, :width, :] + got_ref[k, :width, :].astype(f32)
        den = own_ref[k, width:, :] + got_ref[k, width:, :].astype(f32)
        mixed = proj_ref[:, at] + num / (den + 1e-6)
        center = mixed - jnp.mean(mixed, axis=0, keepdims=True)
        spread = jnp.mean(center * center, axis=0, keepdims=True)
        normed = center * lax.rsqrt(spread + 1e-5) * gains_ref[...]
        out_ref[:, at] = (x_ref[:, at].astype(f32) + jnp.maximum(normed, 0.0)).astype(jnp.bfloat16)


def finish(got, own, proj, gains, x):
    vmem = pl.BlockSpec(memory_space=pltpu.VMEM)
    return pl.pallas_call(
        finish_kernel,
        out_shape=jax.ShapeDtypeStruct(x.shape, jnp.bfloat16),
        in_specs=[vmem] * 5,
        out_specs=vmem,
        compiler_params=GRANT,
        name="finish",
    )(got, own, proj, gains, x)


def flip(x, axes):
    last = 2 ** len(axes) - 1
    return lax.ppermute(x, axes, [(i, i ^ last) for i in range(last + 1)])


def local(x, edge_values, tile_rows, tile_cols, wa, wb, wd, we, edge_gain, ln_gain):
    width, shard = x.shape
    n_tiles, block_len = edge_values.shape[-3], edge_values.shape[-1]
    n_blocks = shard // block_len
    n_za, n_x = lax.axis_size("za"), lax.axis_size("x")
    rows, cols = tile_rows.reshape(-1), tile_cols.reshape(-1)
    tiles = edge_values.reshape(n_tiles, block_len, block_len)
    here = jnp.stack([lax.axis_index(a) for a in ("zb", "yb", "yhi", SRC)]).astype(jnp.int32)

    shard_rows, copies, both = pack(rows, x, block_len, n_za * 2, n_x * 2)
    partner = flip(shard_rows, ("yhi",))
    held = lax.all_to_all(copies, ("za", "ya"), 0, 0).reshape(-1, width, block_len)
    asked, _ = lax.optimization_barrier((cols, shard_rows))
    cols_z = flip(asked, ("zb",))
    cols_y, cols_zy = flip(jnp.stack([asked, cols_z]), ("yb",))
    row_panel = lax.all_to_all(pair(partner, both), ("x", "core"), 0, 0)
    row_panel = row_panel.reshape(n_x * 4, -1, block_len)

    def pick(names):
        owner = names // n_blocks
        place = (owner // 8 * 2 + owner // 2 % 2) * n_blocks + names % n_blocks
        return held.at[place].get(mode="promise_in_bounds")

    got_z = flip(pick(cols_z), ("zb",))
    got_y = flip(pick(cols_y), ("yb",))
    got_zy = flip(pick(cols_zy), ("zb", "yb"))

    parts = tile_sums(
        here, rows, cols, edge_gain, row_panel, held, got_z, got_y, got_zy, tiles, wd, we, wb, n_x * 4
    )
    parts = lax.all_to_all(parts.reshape((n_x * 2, 2) + parts.shape[1:]), ("x", "core"), 0, 0)
    panel = row_panel.reshape((n_x * 2, 2) + row_panel.shape[1:])
    got = flip(far_sums(here, parts, panel, n_blocks), ("yhi",))
    return finish(got, *own_sums(here, parts, panel, x, wa, ln_gain[None]), x)


def solution(mesh):
    n_dst, n_src = mesh.devices.shape
    fine = Mesh(mesh.devices.reshape(n_dst // 8, 2, 2, 2, n_src // 4, 2, 2), AXES)
    in_specs = (
        P(None, AXES), P(DST, SRC, None, None, None), P(DST, SRC, None), P(DST, SRC, None),
        P(), P(), P(), P(), P(), P(),
    )
    return jax.shard_map(local, mesh=fine, in_specs=in_specs, out_specs=P(None, AXES), check_vma=False)
```

```python
import functools

import jax, jax.numpy as jnp
from jax import lax
from jax.sharding import Mesh, PartitionSpec as P
from jax.experimental import pallas as pl
from jax.experimental.pallas import tpu as pltpu

AXES = ("za", "zb", "ya", "yb", "x", "yhi", "core")
DST, SRC = AXES[:4], AXES[4:]
GROUP = 8
CHUNK = 128
BAND = 16
HERE = 4


def pack_kernel(rows_ref, x_ref, shard_ref, spread_ref):
    width, shard = x_ref.shape
    block_len = spread_ref.shape[3]
    n_tiles = rows_ref.shape[0]
    for k in range(shard // block_len):
        block = x_ref[:, k * block_len:(k + 1) * block_len]
        shard_ref[k * width:(k + 1) * width, :] = block
        for n in range(spread_ref.shape[0]):
            spread_ref[n, k] = block
    sub = lax.broadcasted_iota(jnp.int32, (BAND, block_len), 0)
    band = jnp.full((BAND, block_len), -1, jnp.int32)
    for t in range(n_tiles):
        band = jnp.where(sub == t, rows_ref[t], band)
    shard_ref[shard // block_len * width:, :] = band.astype(jnp.float32).astype(shard_ref.dtype)


def pack(rows, x, block_len, copies):
    width, shard = x.shape
    n_blocks = shard // block_len
    vmem = pl.BlockSpec(memory_space=pltpu.VMEM)
    return pl.pallas_call(
        pack_kernel,
        out_shape=(
            jax.ShapeDtypeStruct((n_blocks * width + BAND, block_len), x.dtype),
            jax.ShapeDtypeStruct((copies, n_blocks, width, block_len), x.dtype),
        ),
        in_specs=[pl.BlockSpec(memory_space=pltpu.SMEM), vmem],
        out_specs=(vmem, vmem),
        name="pack",
    )(rows, x)


def pair_kernel(own_ref, partner_ref, out_ref, sem):
    copies = [
        pltpu.make_async_copy(ref, out_ref.at[n, k], sem.at[n, k])
        for n in range(out_ref.shape[0])
        for k, ref in enumerate((own_ref, partner_ref))
    ]
    for copy in copies:
        copy.start()
    for copy in copies:
        copy.wait()


def pair(own, partner, copies):
    vmem = pl.BlockSpec(memory_space=pltpu.VMEM)
    return pl.pallas_call(
        pair_kernel,
        out_shape=jax.ShapeDtypeStruct((copies, 2) + own.shape, own.dtype),
        in_specs=[vmem, vmem],
        out_specs=pl.BlockSpec(memory_space=pl.ANY),
        scratch_shapes=[pltpu.SemaphoreType.DMA((copies, 2))],
        compiler_params=pltpu.CompilerParams(vmem_limit_bytes=32 * 1024 * 1024),
        name="pair",
    )(own, partner)


def tiles_kernel(here_ref, gain_ref, rows_ref, own_ref, got_z_ref, got_y_ref, got_zy_ref, w_ref, wd_ref, we_ref, wb_ref,
                 out_ref, acc, x_scr, d_scr, e_scr, w_scr, lhs_scr, rep_scr):
    n_tiles, block_len, _ = w_ref.shape
    width = wd_ref.shape[0]
    n_blocks = rows_ref.shape[1] // width
    n_groups = width // GROUP
    n_chunks = block_len // CHUNK
    span = GROUP * CHUNK
    f32, bf16 = jnp.float32, jnp.bfloat16
    half = f32(0.5)
    acc[...] = jnp.zeros_like(acc)
    lane = lax.broadcasted_iota(jnp.int32, (block_len, n_chunks * span), 1)
    sub = lax.broadcasted_iota(jnp.int32, (block_len, n_chunks * span), 0)
    rep_scr[...] = (sub == lane // span * CHUNK + lane % CHUNK).astype(f32).astype(bf16)
    lane = lax.broadcasted_iota(jnp.int32, (GROUP, span), 1)
    sub = lax.broadcasted_iota(jnp.int32, (GROUP, span), 0)
    own = (lane // CHUNK == sub).astype(f32)

    for t in range(n_tiles):
        at = slice(t * block_len, (t + 1) * block_len)
        owner, block = here_ref[HERE + t] // n_blocks, here_ref[HERE + t] % n_blocks
        panel = (owner // 4 * 2 + owner % 2) * 2 + ((owner // 2 % 2) ^ here_ref[2])
        x_scr[0, :, at] = rows_ref[panel, pl.ds(pl.multiple_of(block * width, width), width), :]
        owner = here_ref[HERE + n_tiles + t] // n_blocks
        source = ((owner // 2 % 2) ^ here_ref[0]) * 2 + ((owner % 2) ^ here_ref[1])
        place = (owner // 4) * n_blocks + here_ref[HERE + n_tiles + t] % n_blocks
        for k, ref in enumerate((own_ref, got_y_ref, got_z_ref, got_zy_ref)):
            @pl.when(source == k)
            def _(ref=ref, at=at, t=t, k=k):
                x_scr[1, :, at] = ref[place if k == 0 else t]
    d_all = half * jnp.dot(wd_ref[...], x_scr[0], preferred_element_type=f32).astype(bf16).astype(f32)
    b_all = jnp.dot(wb_ref[...], x_scr[1], preferred_element_type=f32).astype(bf16)
    e_all = lax.dot_general(x_scr[1], we_ref[...], (((0,), (1,)), ((), ())), preferred_element_type=f32)
    e_all = (half * e_all.astype(bf16).astype(f32)).astype(bf16)
    for t in range(n_tiles):
        at = slice(t * block_len, (t + 1) * block_len)
        d_scr[t] = d_all[:, at]
        e_scr[t] = e_all[at, :]
        wt = w_ref[t].astype(f32).T
        w_scr[t, 0] = jnp.where(wt != 0, half * wt, -1e35)
        w_scr[t, 1] = jnp.where(wt != 0, -half * wt, -1e35)
        for c in range(n_chunks):
            b_rep = jnp.dot(b_all[:, at], rep_scr[:, c * span:(c + 1) * span], preferred_element_type=f32)
            for g in range(n_groups):
                lhs_scr[t, c, g] = jnp.concatenate([b_rep[g * GROUP:(g + 1) * GROUP] * own, own], axis=0).astype(bf16)

    def tile(t, _):
        owner = here_ref[HERE + t] // n_blocks
        slot = (owner // 4 * 2 + owner % 2) * 2 + ((owner // 2 % 2) ^ here_ref[2])
        for c in range(n_chunks):
            at = slice(c * CHUNK, (c + 1) * CHUNK)
            e_c = e_scr[t, at, :]
            for g in range(n_groups):
                gates = []
                for k in range(GROUP):
                    f = g * GROUP + k
                    gain = gain_ref[f]
                    w_f = w_scr[t, (gain < 0).astype(jnp.int32), at, :]
                    p = jnp.maximum(jnp.abs(gain), 1e-30) * w_f + d_scr[t, f:f + 1, :] + e_c[:, f:f + 1].astype(f32)
                    gates.append((jnp.tanh(p) + 1.0).astype(bf16))
                sums = jnp.dot(lhs_scr[t, c, g], jnp.concatenate(gates, axis=0), preferred_element_type=f32)
                acc[slot, g * GROUP:(g + 1) * GROUP, :] += sums[:GROUP]
                acc[slot, width + g * GROUP:width + (g + 1) * GROUP, :] += sums[GROUP:]
        return 0
    lax.fori_loop(0, n_tiles, tile, 0)
    out_ref[...] = (half * acc[...]).astype(out_ref.dtype)


def tile_sums(here, gain, rows, own, got_z, got_y, got_zy, w, wd, we, wb, n_owners):
    n_tiles, block_len, _ = w.shape
    width = wd.shape[0]
    smem = pl.BlockSpec(memory_space=pltpu.SMEM)
    vmem = pl.BlockSpec(memory_space=pltpu.VMEM)
    n_chunks, n_groups = block_len // CHUNK, width // GROUP
    return pl.pallas_call(
        tiles_kernel,
        out_shape=jax.ShapeDtypeStruct((n_owners, 2 * width, block_len), jnp.bfloat16),
        in_specs=[smem] * 2 + [vmem] * 9,
        out_specs=vmem,
        scratch_shapes=[
            pltpu.VMEM((n_owners, 2 * width, block_len), jnp.float32),
            pltpu.VMEM((2, width, n_tiles * block_len), jnp.bfloat16),
            pltpu.VMEM((n_tiles, width, block_len), jnp.float32),
            pltpu.VMEM((n_tiles, block_len, width), jnp.bfloat16),
            pltpu.VMEM((n_tiles, 2, block_len, block_len), jnp.float32),
            pltpu.VMEM((n_tiles, n_chunks, n_groups, 2 * GROUP, GROUP * CHUNK), jnp.bfloat16),
            pltpu.VMEM((block_len, n_chunks * GROUP * CHUNK), jnp.bfloat16),
        ],
        compiler_params=pltpu.CompilerParams(vmem_limit_bytes=32 * 1024 * 1024),
        name="tile_sums",
    )(here, gain, rows, own, got_z, got_y, got_zy, w, wd, we, wb)


def sums_kernel(flipped, here_ref, parts_ref, band_ref, out_ref):
    n_senders = parts_ref.shape[0]
    n_blocks = out_ref.shape[0]
    f32 = jnp.float32
    first = ((here_ref[3] ^ flipped) * n_blocks).astype(f32)
    named = [band_ref[s, 0].astype(f32) for s in range(n_senders)]
    for k in range(n_blocks):
        total = jnp.zeros(out_ref.shape[1:], f32)
        for s in range(n_senders):
            hit = jnp.max((named[s] == first + float(k)).astype(f32), axis=0, keepdims=True)
            total += parts_ref[s, 0].astype(f32) * hit
        out_ref[k] = total.astype(out_ref.dtype)


def own_kernel(here_ref, parts_ref, band_ref, x_ref, wa_ref, gain_ref, out_ref, proj_ref, gains_ref):
    width = wa_ref.shape[0]
    lane = lax.broadcasted_iota(jnp.int32, (width, width), 1)
    sub = lax.broadcasted_iota(jnp.int32, (width, width), 0)
    gain = jnp.sum(jnp.where(lane == sub, gain_ref[...], 0.0), axis=1, keepdims=True)
    gains_ref[...] = jnp.broadcast_to(gain, gains_ref.shape)
    proj_ref[...] = jnp.dot(wa_ref[...], x_ref[...], preferred_element_type=jnp.float32)
    sums_kernel(0, here_ref, parts_ref, band_ref, out_ref)


def whole(shape):
    return pl.BlockSpec(shape, lambda i: (0,) * len(shape))


def sums_specs(parts, panel, side):
    n, _, depth, block_len = parts.shape
    return [
        pl.BlockSpec(memory_space=pltpu.SMEM),
        pl.BlockSpec((n, 1, depth, block_len), lambda i: (0, side, 0, 0)),
        pl.BlockSpec((n, 1, BAND, block_len), lambda i: (0, 0, panel.shape[2] // BAND - 1, 0)),
    ]


GRANT = pltpu.CompilerParams(vmem_limit_bytes=4 * 1024 * 1024)


def far_sums(here, parts, panel, n_blocks):
    shape = (n_blocks,) + parts.shape[2:]
    return pl.pallas_call(
        functools.partial(sums_kernel, 2),
        grid=(1,),
        out_shape=jax.ShapeDtypeStruct(shape, jnp.bfloat16),
        in_specs=sums_specs(parts, panel, 1),
        out_specs=whole(shape),
        compiler_params=GRANT,
        name="far_sums",
    )(here, parts, panel)


def own_sums(here, parts, panel, x, wa, gain):
    width, shard = x.shape
    shape = (shard // parts.shape[3],) + parts.shape[2:]
    shapes = (shape, x.shape, (width, parts.shape[3]))
    return pl.pallas_call(
        own_kernel,
        grid=(1,),
        out_shape=tuple(jax.ShapeDtypeStruct(a, jnp.float32) for a in shapes),
        in_specs=sums_specs(parts, panel, 0) + [whole(x.shape), whole(wa.shape), whole(gain.shape)],
        out_specs=tuple(whole(a) for a in shapes),
        compiler_params=GRANT,
        name="own_sums",
    )(here, parts, panel, x, wa, gain)


def finish_kernel(got_ref, own_ref, proj_ref, gains_ref, x_ref, out_ref):
    width = x_ref.shape[0]
    n_blocks, _, block_len = own_ref.shape
    f32 = jnp.float32
    for k in range(n_blocks):
        at = slice(k * block_len, (k + 1) * block_len)
        num = own_ref[k, :width, :] + got_ref[k, :width, :].astype(f32)
        den = own_ref[k, width:, :] + got_ref[k, width:, :].astype(f32)
        mixed = proj_ref[:, at] + num / (den + 1e-6)
        center = mixed - jnp.mean(mixed, axis=0, keepdims=True)
        spread = jnp.mean(center * center, axis=0, keepdims=True)
        normed = center * lax.rsqrt(spread + 1e-5) * gains_ref[...]
        out_ref[:, at] = (x_ref[:, at].astype(f32) + jnp.maximum(normed, 0.0)).astype(jnp.bfloat16)


def finish(got, own, proj, gains, x):
    vmem = pl.BlockSpec(memory_space=pltpu.VMEM)
    return pl.pallas_call(
        finish_kernel,
        out_shape=jax.ShapeDtypeStruct(x.shape, jnp.bfloat16),
        in_specs=[vmem] * 5,
        out_specs=vmem,
        compiler_params=GRANT,
        name="finish",
    )(got, own, proj, gains, x)


def flip(x, axes):
    last = 2 ** len(axes) - 1
    return lax.ppermute(x, axes, [(i, i ^ last) for i in range(last + 1)])


def local(x, edge_values, tile_rows, tile_cols, wa, wb, wd, we, edge_gain, ln_gain):
    width, shard = x.shape
    n_tiles, block_len = edge_values.shape[-3], edge_values.shape[-1]
    n_blocks = shard // block_len
    n_za, n_x = lax.axis_size("za"), lax.axis_size("x")
    rows, cols = tile_rows.reshape(-1), tile_cols.reshape(-1)
    tiles = edge_values.reshape(n_tiles, block_len, block_len)
    here = jnp.stack([lax.axis_index(a) for a in ("ya", "yb", "yhi", SRC)]).astype(jnp.int32)
    here = jnp.concatenate([here, rows, cols])

    shard_rows, copies = pack(rows, x, block_len, n_za * 2)
    partner = flip(shard_rows, ("yhi",))
    held = lax.all_to_all(copies, ("za", "zb"), 0, 0).reshape(-1, width, block_len)
    asked, _ = lax.optimization_barrier((cols, shard_rows))
    cols_z = flip(asked, ("ya",))
    cols_y, cols_zy = flip(jnp.stack([asked, cols_z]), ("yb",))
    row_panel = lax.all_to_all(pair(shard_rows, partner, n_x * 2), ("x", "core"), 0, 0)
    row_panel = row_panel.reshape(n_x * 4, -1, block_len)

    def pick(names):
        owner = names // n_blocks
        place = (owner // 4) * n_blocks + names % n_blocks
        return held.at[place].get(mode="promise_in_bounds")

    got_z = flip(pick(cols_z), ("ya",))
    got_y = flip(pick(cols_y), ("yb",))
    got_zy = flip(pick(cols_zy), ("ya", "yb"))

    parts = tile_sums(
        here, edge_gain, row_panel, held, got_z, got_y, got_zy, tiles, wd, we, wb, n_x * 4
    )
    parts = lax.all_to_all(parts.reshape((n_x * 2, 2) + parts.shape[1:]), ("x", "core"), 0, 0)
    panel = row_panel.reshape((n_x * 2, 2) + row_panel.shape[1:])
    got = flip(far_sums(here, parts, panel, n_blocks), ("yhi",))
    return finish(got, *own_sums(here, parts, panel, x, wa, ln_gain[None]), x)


def solution(mesh):
    n_dst, n_src = mesh.devices.shape
    fine = Mesh(mesh.devices.reshape(n_dst // 8, 2, 2, 2, n_src // 4, 2, 2), AXES)
    in_specs = (
        P(None, AXES), P(DST, SRC, None, None, None), P(DST, SRC, None), P(DST, SRC, None),
        P(), P(), P(), P(), P(), P(),
    )
    return jax.shard_map(local, mesh=fine, in_specs=in_specs, out_specs=P(None, AXES), check_vma=False)
```

```python
import functools

import jax, jax.numpy as jnp
from jax import lax
from jax.sharding import Mesh, PartitionSpec as P
from jax.experimental import pallas as pl
from jax.experimental.pallas import tpu as pltpu

AXES = ("za", "zb", "ya", "yb", "x", "yhi", "core")
DST, SRC = AXES[:4], AXES[4:]
GROUP = 8
CHUNK = 128
BAND = 16
HERE = 4


def pack_kernel(rows_ref, x_ref, shard_ref, spread_ref):
    width, shard = x_ref.shape
    block_len = spread_ref.shape[3]
    n_tiles = rows_ref.shape[0]
    for k in range(shard // block_len):
        block = x_ref[:, k * block_len:(k + 1) * block_len]
        shard_ref[k * width:(k + 1) * width, :] = block
        for n in range(spread_ref.shape[0]):
            spread_ref[n, k] = block
    sub = lax.broadcasted_iota(jnp.int32, (BAND, block_len), 0)
    band = jnp.full((BAND, block_len), -1, jnp.int32)
    for t in range(n_tiles):
        band = jnp.where(sub == t, rows_ref[t], band)
    shard_ref[shard // block_len * width:, :] = band.astype(jnp.float32).astype(shard_ref.dtype)


def pack(rows, x, block_len, copies):
    width, shard = x.shape
    n_blocks = shard // block_len
    vmem = pl.BlockSpec(memory_space=pltpu.VMEM)
    return pl.pallas_call(
        pack_kernel,
        out_shape=(
            jax.ShapeDtypeStruct((n_blocks * width + BAND, block_len), x.dtype),
            jax.ShapeDtypeStruct((copies, n_blocks, width, block_len), x.dtype),
        ),
        in_specs=[pl.BlockSpec(memory_space=pltpu.SMEM), vmem],
        out_specs=(vmem, vmem),
        name="pack",
    )(rows, x)


def pair_kernel(own_ref, partner_ref, out_ref, sem):
    copies = [
        pltpu.make_async_copy(ref, out_ref.at[n, k], sem.at[n, k])
        for n in range(out_ref.shape[0])
        for k, ref in enumerate((own_ref, partner_ref))
    ]
    for copy in copies:
        copy.start()
    for copy in copies:
        copy.wait()


def pair(own, partner, copies):
    vmem = pl.BlockSpec(memory_space=pltpu.VMEM)
    return pl.pallas_call(
        pair_kernel,
        out_shape=jax.ShapeDtypeStruct((copies, 2) + own.shape, own.dtype),
        in_specs=[vmem, vmem],
        out_specs=pl.BlockSpec(memory_space=pl.ANY),
        scratch_shapes=[pltpu.SemaphoreType.DMA((copies, 2))],
        compiler_params=pltpu.CompilerParams(vmem_limit_bytes=32 * 1024 * 1024),
        name="pair",
    )(own, partner)


def tiles_kernel(here_ref, gain_ref, rows_ref, own_ref, got_z_ref, got_y_ref, got_zy_ref, w_ref, wd_ref, we_ref, wb_ref,
                 out_ref, acc, x_scr, d_scr, e_scr, w_scr, lhs_scr, rep_scr):
    n_tiles, block_len, _ = w_ref.shape
    width = wd_ref.shape[0]
    n_blocks = rows_ref.shape[1] // width
    n_groups = width // GROUP
    n_chunks = block_len // CHUNK
    span = GROUP * CHUNK
    f32, bf16 = jnp.float32, jnp.bfloat16
    half = f32(0.5)
    acc[...] = jnp.zeros_like(acc)
    lane = lax.broadcasted_iota(jnp.int32, (block_len, n_chunks * span), 1)
    sub = lax.broadcasted_iota(jnp.int32, (block_len, n_chunks * span), 0)
    rep_scr[...] = (sub == lane // span * CHUNK + lane % CHUNK).astype(f32).astype(bf16)
    lane = lax.broadcasted_iota(jnp.int32, (GROUP, span), 1)
    sub = lax.broadcasted_iota(jnp.int32, (GROUP, span), 0)
    own = (lane // CHUNK == sub).astype(f32)

    for t in range(n_tiles):
        at = slice(t * block_len, (t + 1) * block_len)
        owner, block = here_ref[HERE + t] // n_blocks, here_ref[HERE + t] % n_blocks
        panel = (owner // 4 * 2 + owner % 2) * 2 + ((owner // 2 % 2) ^ here_ref[2])
        x_scr[0, :, at] = rows_ref[panel, pl.ds(pl.multiple_of(block * width, width), width), :]
        owner = here_ref[HERE + n_tiles + t] // n_blocks
        source = ((owner // 2 % 2) ^ here_ref[0]) * 2 + ((owner % 2) ^ here_ref[1])
        place = (owner // 4) * n_blocks + here_ref[HERE + n_tiles + t] % n_blocks
        for k, ref in enumerate((own_ref, got_y_ref, got_z_ref, got_zy_ref)):
            @pl.when(source == k)
            def _(ref=ref, at=at, t=t, k=k):
                x_scr[1, :, at] = ref[place if k == 0 else t]
    d_all = half * jnp.dot(wd_ref[...], x_scr[0], preferred_element_type=f32).astype(bf16).astype(f32)
    b_all = jnp.dot(wb_ref[...], x_scr[1], preferred_element_type=f32).astype(bf16)
    e_all = lax.dot_general(x_scr[1], we_ref[...], (((0,), (1,)), ((), ())), preferred_element_type=f32)
    e_all = (half * e_all.astype(bf16).astype(f32)).astype(bf16)
    for t in range(n_tiles):
        at = slice(t * block_len, (t + 1) * block_len)
        d_scr[t] = d_all[:, at]
        e_scr[t] = e_all[at, :]
        wt = w_ref[t].astype(f32).T
        w_scr[t, 0] = jnp.where(wt != 0, half * wt, -1e35)
        w_scr[t, 1] = jnp.where(wt != 0, -half * wt, -1e35)
        for c in range(n_chunks):
            b_rep = jnp.dot(b_all[:, at], rep_scr[:, c * span:(c + 1) * span], preferred_element_type=f32)
            for g in range(n_groups):
                lhs_scr[t, c, g] = jnp.concatenate([b_rep[g * GROUP:(g + 1) * GROUP] * own, own], axis=0).astype(bf16)

    def tile(t, _):
        owner = here_ref[HERE + t] // n_blocks
        slot = (owner // 4 * 2 + owner % 2) * 2 + ((owner // 2 % 2) ^ here_ref[2])
        for c in range(n_chunks):
            at = slice(c * CHUNK, (c + 1) * CHUNK)
            e_c = e_scr[t, at, :]
            for g in range(n_groups):
                gates = []
                for k in range(GROUP):
                    f = g * GROUP + k
                    gain = gain_ref[f]
                    w_f = w_scr[t, (gain < 0).astype(jnp.int32), at, :]
                    p = jnp.abs(gain) * w_f + d_scr[t, f:f + 1, :] + e_c[:, f:f + 1].astype(f32)
                    gates.append((jnp.tanh(p) + 1.0).astype(bf16))
                sums = jnp.dot(lhs_scr[t, c, g], jnp.concatenate(gates, axis=0), preferred_element_type=f32)
                acc[slot, g * GROUP:(g + 1) * GROUP, :] += sums[:GROUP]
                acc[slot, width + g * GROUP:width + (g + 1) * GROUP, :] += sums[GROUP:]
        return 0
    lax.fori_loop(0, n_tiles, tile, 0)
    out_ref[...] = (half * acc[...]).astype(out_ref.dtype)


def tile_sums(here, gain, rows, own, got_z, got_y, got_zy, w, wd, we, wb, n_owners):
    n_tiles, block_len, _ = w.shape
    width = wd.shape[0]
    smem = pl.BlockSpec(memory_space=pltpu.SMEM)
    vmem = pl.BlockSpec(memory_space=pltpu.VMEM)
    n_chunks, n_groups = block_len // CHUNK, width // GROUP
    return pl.pallas_call(
        tiles_kernel,
        out_shape=jax.ShapeDtypeStruct((n_owners, 2 * width, block_len), jnp.bfloat16),
        in_specs=[smem] * 2 + [vmem] * 9,
        out_specs=vmem,
        scratch_shapes=[
            pltpu.VMEM((n_owners, 2 * width, block_len), jnp.float32),
            pltpu.VMEM((2, width, n_tiles * block_len), jnp.bfloat16),
            pltpu.VMEM((n_tiles, width, block_len), jnp.float32),
            pltpu.VMEM((n_tiles, block_len, width), jnp.bfloat16),
            pltpu.VMEM((n_tiles, 2, block_len, block_len), jnp.float32),
            pltpu.VMEM((n_tiles, n_chunks, n_groups, 2 * GROUP, GROUP * CHUNK), jnp.bfloat16),
            pltpu.VMEM((block_len, n_chunks * GROUP * CHUNK), jnp.bfloat16),
        ],
        compiler_params=pltpu.CompilerParams(vmem_limit_bytes=32 * 1024 * 1024),
        name="tile_sums",
    )(here, gain, rows, own, got_z, got_y, got_zy, w, wd, we, wb)


def sums_kernel(flipped, here_ref, parts_ref, band_ref, out_ref):
    n_senders = parts_ref.shape[0]
    n_blocks = out_ref.shape[0]
    f32 = jnp.float32
    first = ((here_ref[3] ^ flipped) * n_blocks).astype(f32)
    named = [band_ref[s, 0].astype(f32) for s in range(n_senders)]
    for k in range(n_blocks):
        total = jnp.zeros(out_ref.shape[1:], f32)
        for s in range(n_senders):
            hit = jnp.max((named[s] == first + float(k)).astype(f32), axis=0, keepdims=True)
            total += parts_ref[s, 0].astype(f32) * hit
        out_ref[k] = total.astype(out_ref.dtype)


def own_kernel(here_ref, parts_ref, band_ref, x_ref, wa_ref, gain_ref, out_ref, proj_ref, gains_ref):
    width = wa_ref.shape[0]
    lane = lax.broadcasted_iota(jnp.int32, (width, width), 1)
    sub = lax.broadcasted_iota(jnp.int32, (width, width), 0)
    gain = jnp.sum(jnp.where(lane == sub, gain_ref[...], 0.0), axis=1, keepdims=True)
    gains_ref[...] = jnp.broadcast_to(gain, gains_ref.shape)
    proj_ref[...] = jnp.dot(wa_ref[...], x_ref[...], preferred_element_type=jnp.float32)
    sums_kernel(0, here_ref, parts_ref, band_ref, out_ref)


def whole(shape):
    return pl.BlockSpec(shape, lambda i: (0,) * len(shape))


def sums_specs(parts, panel, side):
    n, _, depth, block_len = parts.shape
    return [
        pl.BlockSpec(memory_space=pltpu.SMEM),
        pl.BlockSpec((n, 1, depth, block_len), lambda i: (0, side, 0, 0)),
        pl.BlockSpec((n, 1, BAND, block_len), lambda i: (0, 0, panel.shape[2] // BAND - 1, 0)),
    ]


GRANT = pltpu.CompilerParams(vmem_limit_bytes=4 * 1024 * 1024)


def far_sums(here, parts, panel, n_blocks):
    shape = (n_blocks,) + parts.shape[2:]
    return pl.pallas_call(
        functools.partial(sums_kernel, 2),
        grid=(1,),
        out_shape=jax.ShapeDtypeStruct(shape, jnp.bfloat16),
        in_specs=sums_specs(parts, panel, 1),
        out_specs=whole(shape),
        compiler_params=GRANT,
        name="far_sums",
    )(here, parts, panel)


def own_sums(here, parts, panel, x, wa, gain):
    width, shard = x.shape
    shape = (shard // parts.shape[3],) + parts.shape[2:]
    shapes = (shape, x.shape, (width, parts.shape[3]))
    return pl.pallas_call(
        own_kernel,
        grid=(1,),
        out_shape=tuple(jax.ShapeDtypeStruct(a, jnp.float32) for a in shapes),
        in_specs=sums_specs(parts, panel, 0) + [whole(x.shape), whole(wa.shape), whole(gain.shape)],
        out_specs=tuple(whole(a) for a in shapes),
        compiler_params=GRANT,
        name="own_sums",
    )(here, parts, panel, x, wa, gain)


def finish_kernel(got_ref, own_ref, proj_ref, gains_ref, x_ref, out_ref):
    width = x_ref.shape[0]
    n_blocks, _, block_len = own_ref.shape
    f32 = jnp.float32
    for k in range(n_blocks):
        at = slice(k * block_len, (k + 1) * block_len)
        num = own_ref[k, :width, :] + got_ref[k, :width, :].astype(f32)
        den = own_ref[k, width:, :] + got_ref[k, width:, :].astype(f32)
        mixed = proj_ref[:, at] + num / (den + 1e-6)
        center = mixed - jnp.mean(mixed, axis=0, keepdims=True)
        spread = jnp.mean(center * center, axis=0, keepdims=True)
        normed = center * lax.rsqrt(spread + 1e-5) * gains_ref[...]
        out_ref[:, at] = (x_ref[:, at].astype(f32) + jnp.maximum(normed, 0.0)).astype(jnp.bfloat16)


def finish(got, own, proj, gains, x):
    vmem = pl.BlockSpec(memory_space=pltpu.VMEM)
    return pl.pallas_call(
        finish_kernel,
        out_shape=jax.ShapeDtypeStruct(x.shape, jnp.bfloat16),
        in_specs=[vmem] * 5,
        out_specs=vmem,
        compiler_params=GRANT,
        name="finish",
    )(got, own, proj, gains, x)


def flip(x, axes):
    last = 2 ** len(axes) - 1
    return lax.ppermute(x, axes, [(i, i ^ last) for i in range(last + 1)])


def local(x, edge_values, tile_rows, tile_cols, wa, wb, wd, we, edge_gain, ln_gain):
    width, shard = x.shape
    n_tiles, block_len = edge_values.shape[-3], edge_values.shape[-1]
    n_blocks = shard // block_len
    n_za, n_x = lax.axis_size("za"), lax.axis_size("x")
    rows, cols = tile_rows.reshape(-1), tile_cols.reshape(-1)
    tiles = edge_values.reshape(n_tiles, block_len, block_len)
    here = jnp.stack([lax.axis_index(a) for a in ("ya", "yb", "yhi", SRC)]).astype(jnp.int32)
    here = jnp.concatenate([here, rows, cols])
    gain = jnp.where(edge_gain < 0, jnp.minimum(edge_gain, -1e-30), jnp.maximum(edge_gain, 1e-30))

    shard_rows, copies = pack(rows, x, block_len, n_za * 2)
    partner = flip(shard_rows, ("yhi",))
    held = lax.all_to_all(copies, ("za", "zb"), 0, 0).reshape(-1, width, block_len)
    asked, _ = lax.optimization_barrier((cols, shard_rows))
    cols_y = flip(asked, ("yb",))
    cols_z, cols_zy = flip(jnp.stack([asked, cols_y]), ("ya",))
    row_panel = lax.all_to_all(pair(shard_rows, partner, n_x * 2), ("x", "core"), 0, 0)
    row_panel = row_panel.reshape(n_x * 4, -1, block_len)

    def pick(names):
        owner = names // n_blocks
        place = (owner // 4) * n_blocks + names % n_blocks
        return held.at[place].get(mode="promise_in_bounds")

    got_z = flip(pick(cols_z), ("ya",))
    got_y = flip(pick(cols_y), ("yb",))
    got_zy = flip(pick(cols_zy), ("ya", "yb"))

    parts = tile_sums(
        here, gain, row_panel, held, got_z, got_y, got_zy, tiles, wd, we, wb, n_x * 4
    )
    parts = lax.all_to_all(parts.reshape((n_x * 2, 2) + parts.shape[1:]), ("x", "core"), 0, 0)
    panel = row_panel.reshape((n_x * 2, 2) + row_panel.shape[1:])
    got = flip(far_sums(here, parts, panel, n_blocks), ("yhi",))
    return finish(got, *own_sums(here, parts, panel, x, wa, ln_gain[None]), x)


def solution(mesh):
    n_dst, n_src = mesh.devices.shape
    fine = Mesh(mesh.devices.reshape(n_dst // 8, 2, 2, 2, n_src // 4, 2, 2), AXES)
    in_specs = (
        P(None, AXES), P(DST, SRC, None, None, None), P(DST, SRC, None), P(DST, SRC, None),
        P(), P(), P(), P(), P(), P(),
    )
    return jax.shard_map(local, mesh=fine, in_specs=in_specs, out_specs=P(None, AXES), check_vma=False)
```
